256 devices in a mesh: row: 16 (over y, x), col: 16 (over z, core).
Axes of the slice: x: 4, y: 4, z: 8, core: 2. Of those that a mesh axis runs over, the one named last changes fastest.
Arguments:
- gradients: float32 [2, 8192, 28672], P(None, 'row', 'col'), may hold values from -8 to 8
- sketch: float32 [28672, 256], P('col'), may hold values from -0.03125 to 0.03125
Outputs:
- projection_basis: float32 [2, 8192, 256], P(None, ('row', 'col'))
- projected: float32 [2, 256, 28672], P(None, 'row', 'col')
The draws below stay inside these ranges and needn't reach their ends.
All inputs are finite; a program needn't handle non-finite values.
Results may differ from the reference program's by a relative error of at most 0.0039.
Values sent between devices are 32-bit elements; how exact they have to be, the bound alone decides.
No kernel may reach another device: no remote copies, remote signals or barrier semaphores. Data moves between devices by JAX's collectives and lax.ppermute only.
A program may use at most 256 MiB of HBM per device.

```python
import jax
import jax.numpy as jnp
from jax import lax

M = 8192
N = 28672
R = 256
GRADS = 2


def draw_gradients(key, part):
    key = jax.random.fold_in(key, 11)
    noise_key, left_key, right_key = jax.random.split(key, 3)
    noise = jnp.clip(jax.random.normal(noise_key, (GRADS, M, N), jnp.float32), -4.0, 4.0)
    left = jnp.clip(jax.random.normal(left_key, (GRADS, M), jnp.float32), -2.5, 2.5)
    right = jnp.clip(jax.random.normal(right_key, (GRADS, N), jnp.float32), -2.5, 2.5)
    return noise + 0.6 * left[:, :, None] * right[:, None, :]


def block_levels(rng, dims, shards, smallest, high):
    gain = 1.0
    for position, shards_of in shards:
        heights = jax.random.uniform(jax.random.fold_in(jax.random.fold_in(rng, 6), position), (shards_of,), jnp.float32, smallest / len(shards), high / len(shards))
        gain = gain * jnp.repeat(jnp.exp(heights), dims[position] // shards_of).reshape((-1,) + (1,) * (len(dims) - 1 - position))
    return gain


def normal_values(stream_key, extent, deviation, limit, cuts=(), dtype=jnp.bfloat16):
    entries = jax.random.normal(stream_key, extent, jnp.float32) * deviation
    if len(cuts) > 0:
        entries = block_levels(stream_key, extent, cuts, -0.22, 0.18) * entries
    return jnp.clip(entries, min=-limit, max=limit).astype(dtype)


def setup_inputs(seed: int = 0) -> dict:
    arg_keys = jax.random.split(jax.random.key(seed), 3)
    gradients = draw_gradients(jax.random.fold_in(arg_keys[2], 71), 0)
    sketch = normal_values(arg_keys[1], (N, R), N ** -0.5, 0.03125, ((0, 16),), jnp.float32)
    return {"gradients": gradients, "sketch": sketch}


def orthonormal(matrix):
    factor_q, factor_r = jnp.linalg.qr(matrix)
    signs = jnp.sign(jnp.diagonal(factor_r, axis1=-2, axis2=-1))
    return factor_q * signs[..., None, :]

def reference(gradients, sketch):
    precise = lax.Precision.HIGHEST
    first = jnp.einsum('bmn,nr->bmr', gradients, sketch, precision=precise)
    basis_one = orthonormal(first)
    pulled = jnp.einsum('bmn,bmr->bnr', gradients, basis_one, precision=precise)
    second = jnp.einsum('bmn,bnr->bmr', gradients, pulled, precision=precise)
    basis_two = orthonormal(second)
    projected = jnp.einsum('bmr,bmn->brn', basis_two, gradients, precision=precise)
    scale = jnp.sqrt(jnp.float32(M))
    return (basis_two * scale, projected)
```

```python
import jax
import jax.numpy as jnp
from jax import lax
from jax.experimental import pallas as pl
from jax.experimental.pallas import tpu as pltpu
from jax.sharding import PartitionSpec as P

FULL = lax.Precision.HIGHEST
FAST = lax.Precision.HIGH
CORES = 2
PANEL = 32


def inverse_factor_kernel(gram_ref, out_ref, work_ref):
    grads, rank, _ = gram_ref.shape
    for g in range(grads):
        work_ref[g] = gram_ref[g]
    rows = lax.broadcasted_iota(jnp.int32, (PANEL, rank), 0)
    cols = lax.broadcasted_iota(jnp.int32, (PANEL, rank), 1)
    for lo in range(0, rank, PANEL):
        hi = lo + PANEL
        left = [work_ref[g, lo:hi, :] for g in range(grads)]
        right = [jnp.where(cols == rows + lo, 1.0, 0.0) for g in range(grads)]
        for k in range(PANEL):
            for g in range(grads):
                column = left[g][:, lo + k:lo + k + 1]
                inverse = lax.rsqrt(column[k:k + 1, :])
                left_row = left[g][k:k + 1, :] * inverse
                right_row = right[g][k:k + 1, :] * inverse
                factor = column * inverse
                left[g] = jnp.where(rows > k, left[g] - factor * left_row, jnp.where(rows == k, left_row, left[g]))
                right[g] = jnp.where(rows > k, right[g] - factor * right_row, jnp.where(rows == k, right_row, right[g]))
        inside = (cols >= lo) & (cols < hi)
        for g in range(grads):
            whole = jnp.where(inside, right[g], left[g])
            out_ref[g, lo:hi, :] = jnp.where(cols < hi, whole, 0.0)
            if hi < rank:
                update = lax.dot_general(left[g], whole, (((0,), (0,)), ((), ())), precision=FULL, preferred_element_type=jnp.float32)
                places = lax.broadcasted_iota(jnp.int32, (rank - hi, rank), 1)
                kept = jnp.where((places >= lo) & (places < hi), 0.0, work_ref[g, hi:, :])
                work_ref[g, hi:, :] = kept - update[hi:]


def inverse_factor(gram):
    return pl.pallas_call(
        inverse_factor_kernel,
        out_shape=jax.ShapeDtypeStruct(gram.shape, jnp.float32),
        in_specs=[pl.BlockSpec(memory_space=pltpu.VMEM)],
        out_specs=pl.BlockSpec(memory_space=pltpu.VMEM),
        scratch_shapes=[pltpu.VMEM(gram.shape, jnp.float32)],
        compiler_params=pltpu.CompilerParams(vmem_limit_bytes=32 * 2**20),
    )(gram)


def swap_core(value):
    size = lax.axis_size("col")
    return lax.ppermute(value, "col", [(i, i ^ 1) for i in range(size)])


def chips(value):
    size = lax.axis_size("col")
    groups = [list(range(core, size, CORES)) for core in range(CORES)]
    return lax.all_to_all(value, "col", 0, 0, axis_index_groups=groups, tiled=True)


def spread(value, count):
    return jnp.broadcast_to(value[None], (count,) + value.shape)


def both_cores(value, axis):
    other = swap_core(value)
    core = lax.axis_index("col") % CORES
    return jnp.stack([jnp.where(core == 0, value, other), jnp.where(core == 0, other, value)], axis)


def half_sum(value, axis):
    core = lax.axis_index("col") % CORES
    mine = lax.dynamic_index_in_dim(value, core, axis, keepdims=False)
    return mine + swap_core(lax.dynamic_index_in_dim(value, 1 - core, axis, keepdims=False))


def shards(gradients, sketch):
    grads, depth, width = gradients.shape
    rank = sketch.shape[1]
    row_size, col_size = lax.axis_size("row"), lax.axis_size("col")
    chip_count = col_size // CORES
    part = depth // col_size
    slab = width // row_size
    total_rows = depth * row_size

    def halve(value):
        pieces = value.reshape(grads, chip_count, CORES, part, rank)
        return jnp.swapaxes(half_sum(pieces, 2), 0, 1)

    def join(pieces):
        whole = both_cores(pieces, 2)
        return jnp.moveaxis(whole, 0, 1).reshape(grads, depth, rank)

    first_part = jnp.einsum("bmn,nr->bmr", gradients, sketch, precision=FAST)
    first_mine = jnp.sum(chips(halve(first_part)), 0)
    first = join(chips(spread(first_mine, chip_count)))

    pulled_part = jnp.einsum("bmn,bmr->bnr", gradients, first, precision=FAST)
    pulled_part = jnp.swapaxes(pulled_part.reshape(grads, row_size, slab, rank), 0, 1)
    pulled_mine = jnp.sum(lax.all_to_all(pulled_part, "row", 0, 0, tiled=True), 0)
    pulled = lax.all_to_all(spread(pulled_mine, row_size), "row", 0, 0, tiled=True)
    pulled = jnp.swapaxes(pulled, 0, 1).reshape(grads, width, rank)

    second_part = jnp.einsum("bmn,bnr->bmr", gradients, pulled, precision=FAST)
    gram_part = half_sum(jnp.einsum("bnr,bns->brs", pulled, pulled, precision=FULL), 0)
    packed = jnp.concatenate([halve(second_part).reshape(chip_count, grads * part, rank), gram_part.reshape(chip_count, rank // chip_count, rank)], 1)
    packed_mine = jnp.sum(chips(packed), 0)
    packed = chips(spread(packed_mine, chip_count))
    raw = join(packed[:, :grads * part].reshape(chip_count, grads, part, rank))
    gram = both_cores(packed[:, grads * part:].reshape(rank, rank), 0)

    balanced = jnp.einsum("bmr,bsr->bms", raw, inverse_factor(gram), precision=FULL)
    chosen = lax.dynamic_index_in_dim(balanced, lax.axis_index("col") % CORES, 0, keepdims=False)
    gram_part = jnp.einsum("mr,ms->rs", chosen, chosen, precision=FULL)
    gram_part = gram_part.reshape(row_size, rank // row_size, rank)
    gram_mine = jnp.sum(lax.all_to_all(gram_part, "row", 0, 0, tiled=True), 0)
    gram = lax.all_to_all(spread(gram_mine, row_size), "row", 0, 0, tiled=True).reshape(rank, rank)
    gram = both_cores(gram, 0)
    basis = jnp.einsum("bmr,bsr->bms", balanced, inverse_factor(gram), precision=FULL)

    terms = jnp.einsum("bmr,bmn->brn", basis, gradients, precision=FAST)
    terms = jnp.swapaxes(terms.reshape(grads, row_size, rank // row_size, width), 0, 1)
    projected = jnp.sum(lax.all_to_all(terms, "row", 0, 0, tiled=True), 0)
    basis_mine = lax.dynamic_slice_in_dim(basis, lax.axis_index("col") * part, part, 1)
    return (basis_mine * jnp.sqrt(jnp.float32(total_rows)), projected)


def solution(mesh):
    in_specs = (P(None, "row", "col"), P("col", None))
    out_specs = (P(None, ("row", "col"), None), P(None, "row", "col"))
    return jax.shard_map(shards, mesh=mesh, in_specs=in_specs, out_specs=out_specs, check_vma=False)
```

```python
import jax
import jax.numpy as jnp
from jax import lax
from jax.experimental import pallas as pl
from jax.experimental.pallas import tpu as pltpu
from jax.sharding import PartitionSpec as P

FULL = lax.Precision.HIGHEST
FAST = lax.Precision.HIGH
CORES = 2
PANEL = 32
GROUP = 8
LANES = 128
SIDE = 4
CUBE = (0, 2, 1, 3)


def inverse_factor_kernel(gram_ref, out_ref, work_ref):
    grads, rank, _ = gram_ref.shape
    for g in range(grads):
        work_ref[g] = gram_ref[g]
    rows = lax.broadcasted_iota(jnp.int32, (PANEL, LANES), 0)
    lanes = lax.broadcasted_iota(jnp.int32, (PANEL, LANES), 1)

    def fill(value):
        return jnp.broadcast_to(value, (PANEL, LANES))

    for lo in range(0, rank, PANEL):
        hi = lo + PANEL
        tile, offset = lo // LANES, lo % LANES
        left = [[work_ref[g, lo:hi, i:i + LANES] for i in range(0, rank, LANES)] for g in range(grads)]
        right = [jnp.where(lanes == rows + offset, 1.0, 0.0) for g in range(grads)]
        for start in range(0, PANEL, GROUP):
            columns = [[fill(left[g][tile][:, offset + start + j:offset + start + j + 1]) for j in range(GROUP)] for g in range(grads)]
            for j in range(GROUP):
                k = start + j
                for g in range(grads):
                    inverse = lax.rsqrt(fill(columns[g][j][k:k + 1, :]))
                    factor = columns[g][j] * inverse
                    for i in range(j + 1, GROUP):
                        columns[g][i] = columns[g][i] - factor * fill(factor[start + i:start + i + 1, :])

                    def eliminate(value):
                        pivot = fill(value[k:k + 1, :]) * inverse
                        return jnp.where(rows > k, value - factor * pivot, jnp.where(rows == k, pivot, value))

                    left[g] = [eliminate(value) for value in left[g]]
                    right[g] = eliminate(right[g])
        inside = (lanes >= offset) & (lanes < offset + PANEL)
        for g in range(grads):
            whole = [jnp.where(inside, right[g], value) if i == tile else value for i, value in enumerate(left[g])]
            for i, value in enumerate(whole):
                known = jnp.where(lanes + i * LANES < hi, value, 0.0)
                out_ref[g, lo:hi, i * LANES:(i + 1) * LANES] = known
            if hi < rank:
                update = lax.dot_general(jnp.concatenate(left[g], 1), jnp.concatenate(whole, 1), (((0,), (0,)), ((), ())), precision=FULL, preferred_element_type=jnp.float32)
                places = lax.broadcasted_iota(jnp.int32, (rank - hi, rank), 1)
                kept = jnp.where((places >= lo) & (places < hi), 0.0, work_ref[g, hi:, :])
                work_ref[g, hi:, :] = kept - update[hi:]


def inverse_factor(gram):
    return pl.pallas_call(
        inverse_factor_kernel,
        out_shape=jax.ShapeDtypeStruct(gram.shape, jnp.float32),
        in_specs=[pl.BlockSpec(memory_space=pltpu.VMEM)],
        out_specs=pl.BlockSpec(memory_space=pltpu.VMEM),
        scratch_shapes=[pltpu.VMEM(gram.shape, jnp.float32)],
        compiler_params=pltpu.CompilerParams(vmem_limit_bytes=32 * 2**20),
    )(gram)


def swap_core(value):
    size = lax.axis_size("col")
    return lax.ppermute(value, "col", [(i, i ^ 1) for i in range(size)])


def chips(value):
    size = lax.axis_size("col")
    groups = [list(range(core, size, CORES)) for core in range(CORES)]
    return lax.all_to_all(value, "col", 0, 0, axis_index_groups=groups, tiled=True)


def spread(value, count):
    return jnp.broadcast_to(value[None], (count,) + value.shape)


def both_cores(value, axis):
    other = swap_core(value)
    core = lax.axis_index("col") % CORES
    return jnp.stack([jnp.where(core == 0, value, other), jnp.where(core == 0, other, value)], axis)


def half_sum(value, axis):
    core = lax.axis_index("col") % CORES
    mine = lax.dynamic_index_in_dim(value, core, axis, keepdims=False)
    return mine + swap_core(lax.dynamic_index_in_dim(value, 1 - core, axis, keepdims=False))


def cube_partner(axis):
    pairs = []
    for y in range(SIDE):
        for x in range(SIDE):
            other = (y, x ^ 1), (y, SIDE - 1 - x), (y ^ 1, x), (SIDE - 1 - y, x)
            pairs.append((SIDE * y + x, SIDE * other[axis][0] + other[axis][1]))
    return pairs


def cube_bits():
    place = lax.axis_index("row")
    bits = []
    for digit in (place % SIDE, place // SIDE):
        bits += [(digit ^ (digit >> 1)) & 1, digit >> 1]
    return bits


def cube_order(quarter):
    return [CUBE[(quarter + step) % len(CUBE)] for step in range(len(CUBE))]


def scatter_sum(quarters):
    bits = cube_bits()
    for step in range(len(CUBE)):
        sent = []
        for q, value in enumerate(quarters):
            axis = cube_order(q)[step]
            half = value.shape[0] // 2
            away = lax.dynamic_slice_in_dim(value, (1 - bits[axis]) * half, half, 0)
            sent.append(lax.ppermute(away, "row", cube_partner(axis)))
        for q, value in enumerate(quarters):
            half = value.shape[0] // 2
            kept = lax.dynamic_slice_in_dim(value, bits[cube_order(q)[step]] * half, half, 0)
            quarters[q] = kept + sent[q]
    return quarters


def cube_places(quarter):
    order = cube_order(quarter)
    places = [0] * SIDE**2
    for place in range(SIDE**2):
        bits = []
        for digit in (place % SIDE, place // SIDE):
            bits += [(digit ^ (digit >> 1)) & 1, digit >> 1]
        position = 0
        for axis in order:
            position = 2 * position + bits[axis]
        places[position] = place
    return places


def gather(quarters):
    bits = cube_bits()
    for step in reversed(range(len(CUBE))):
        got = [lax.ppermute(value, "row", cube_partner(cube_order(q)[step])) for q, value in enumerate(quarters)]
        for q, value in enumerate(quarters):
            high = bits[cube_order(q)[step]] == 1
            quarters[q] = jnp.concatenate([jnp.where(high, got[q], value), jnp.where(high, value, got[q])], 0)
    return quarters


def shards(gradients, sketch):
    grads, depth, width = gradients.shape
    rank = sketch.shape[1]
    row_size, col_size = lax.axis_size("row"), lax.axis_size("col")
    chip_count = col_size // CORES
    part = depth // col_size
    slab = width // row_size
    total_rows = depth * row_size

    def halve(value):
        pieces = value.reshape(grads, chip_count, CORES, part, rank)
        return jnp.swapaxes(half_sum(pieces, 2), 0, 1)

    def join(pieces):
        whole = both_cores(pieces, 2)
        return jnp.moveaxis(whole, 0, 1).reshape(grads, depth, rank)

    first_part = jnp.einsum("bmn,nr->bmr", gradients, sketch, precision=FAST)
    first_mine = jnp.sum(chips(halve(first_part)), 0)
    first = join(chips(spread(first_mine, chip_count)))

    pulled_part = jnp.einsum("bmn,bmr->bnr", gradients, first, precision=FAST)
    half = width // 2
    quarters = scatter_sum([pulled_part[q // 2, q % 2 * half:(q % 2 + 1) * half] for q in range(2 * grads)])
    pulled = jnp.concatenate(gather(quarters), 0).reshape(grads, width, rank)

    second_part = jnp.einsum("bmn,bnr->bmr", gradients, pulled, precision=FAST)
    gram_part = half_sum(jnp.einsum("bnr,bns->brs", pulled, pulled, precision=FULL), 0)
    packed = jnp.concatenate([halve(second_part).reshape(chip_count, grads * part, rank), gram_part.reshape(chip_count, rank // chip_count, rank)], 1)
    packed_mine = jnp.sum(chips(packed), 0)
    packed = chips(spread(packed_mine, chip_count))
    raw = join(packed[:, :grads * part].reshape(chip_count, grads, part, rank))
    gram = both_cores(packed[:, grads * part:].reshape(rank, rank), 0)

    balanced = jnp.einsum("bmr,bsr->bms", raw, inverse_factor(gram), precision=FULL)
    chosen = lax.dynamic_index_in_dim(balanced, lax.axis_index("col") % CORES, 0, keepdims=False)
    gram_part = jnp.einsum("mr,ms->rs", chosen, chosen, precision=FULL)
    gram_part = gram_part.reshape(row_size, rank // row_size, rank)
    gram_mine = jnp.sum(lax.all_to_all(gram_part, "row", 0, 0, tiled=True), 0)
    gram = lax.all_to_all(spread(gram_mine, row_size), "row", 0, 0, tiled=True).reshape(rank, rank)
    gram = both_cores(gram, 0)
    basis = jnp.einsum("bmr,bsr->bms", balanced, inverse_factor(gram), precision=FULL)

    quarters = []
    for q in range(2 * grads):
        terms = jnp.einsum("mr,mn->rn", basis[q // 2], gradients[q // 2, :, q % 2 * half:(q % 2 + 1) * half], precision=FAST)
        blocks = terms.reshape(row_size, rank // row_size, half)
        quarters.append(jnp.concatenate([blocks[i] for i in cube_places(q)], 0))
    quarters = scatter_sum(quarters)
    projected = jnp.stack([jnp.concatenate(quarters[2 * g:2 * g + 2], 1) for g in range(grads)])
    basis_mine = lax.dynamic_slice_in_dim(basis, lax.axis_index("col") * part, part, 1)
    return (basis_mine * jnp.sqrt(jnp.float32(total_rows)), projected)


def solution(mesh):
    in_specs = (P(None, "row", "col"), P("col", None))
    out_specs = (P(None, ("row", "col"), None), P(None, "row", "col"))
    return jax.shard_map(shards, mesh=mesh, in_specs=in_specs, out_specs=out_specs, check_vma=False)
```

```python
import functools

import jax
import jax.numpy as jnp
from jax import lax
from jax.experimental import pallas as pl
from jax.experimental.pallas import tpu as pltpu
from jax.sharding import PartitionSpec as P

FULL = lax.Precision.HIGHEST
CORES = 2
PANEL = 32
GROUP = 8
LANES = 128
SIDE = 4
CUBE = (0, 2, 1, 3)
BLOCK = 16
ROWS = 128
NEAR = (((1,), (0,)), ((), ()))
FAR = (((1,), (1,)), ((), ()))
TALL = (((0,), (0,)), ((), ()))
SMEM = pl.BlockSpec(memory_space=pltpu.SMEM)
VMEM = pl.BlockSpec(memory_space=pltpu.VMEM)


def split(value):
    high = value.astype(jnp.bfloat16)
    return (high, (value - high.astype(jnp.float32)).astype(jnp.bfloat16))


def triple(left, right, dims):
    def dot(a, b):
        return lax.dot_general(a, b, dims, preferred_element_type=jnp.float32)

    return dot(left[0], right[0]) + dot(left[0], right[1]) + dot(left[1], right[0])


def exact(left, right, dims):
    return lax.dot_general(left, right, dims, precision=FULL, preferred_element_type=jnp.float32)


def full_block(shape):
    return pl.BlockSpec(shape, lambda *_: (0,) * len(shape))


def params(grid):
    return pltpu.CompilerParams(dimension_semantics=("arbitrary",) * grid, vmem_limit_bytes=48 * 2**20)


def invert_factor(work_ref, out_ref):
    grads, rank, _ = work_ref.shape
    rows = lax.broadcasted_iota(jnp.int32, (PANEL, LANES), 0)
    lanes = lax.broadcasted_iota(jnp.int32, (PANEL, LANES), 1)

    def fill(value):
        return jnp.broadcast_to(value, (PANEL, LANES))

    for lo in range(0, rank, PANEL):
        hi = lo + PANEL
        tile, offset = lo // LANES, lo % LANES
        left = [[work_ref[g, lo:hi, i:i + LANES] for i in range(0, rank, LANES)] for g in range(grads)]
        right = [jnp.where(lanes == rows + offset, 1.0, 0.0) for g in range(grads)]
        for start in range(0, PANEL, GROUP):
            columns = [[fill(left[g][tile][:, offset + start + j:offset + start + j + 1]) for j in range(GROUP)] for g in range(grads)]
            for j in range(GROUP):
                k = start + j
                for g in range(grads):
                    inverse = lax.rsqrt(fill(columns[g][j][k:k + 1, :]))
                    factor = columns[g][j] * inverse
                    for i in range(j + 1, GROUP):
                        columns[g][i] = columns[g][i] - factor * fill(factor[start + i:start + i + 1, :])

                    def eliminate(value):
                        pivot = fill(value[k:k + 1, :]) * inverse
                        return jnp.where(rows > k, value - factor * pivot, jnp.where(rows == k, pivot, value))

                    left[g] = [eliminate(value) for value in left[g]]
                    right[g] = eliminate(right[g])
        inside = (lanes >= offset) & (lanes < offset + PANEL)
        for g in range(grads):
            whole = [jnp.where(inside, right[g], value) if i == tile else value for i, value in enumerate(left[g])]
            for i, value in enumerate(whole):
                known = jnp.where(lanes + i * LANES < hi, value, 0.0)
                out_ref[g, lo:hi, i * LANES:(i + 1) * LANES] = known
            if hi < rank:
                update = exact(jnp.concatenate(left[g], 1), jnp.concatenate(whole, 1), TALL)
                places = lax.broadcasted_iota(jnp.int32, (rank - hi, rank), 1)
                kept = jnp.where((places >= lo) & (places < hi), 0.0, work_ref[g, hi:, :])
                work_ref[g, hi:, :] = kept - update[hi:]


def place_rows(out_ref, index, part, share, core, mine_ref, other_ref):
    chips = mine_ref.shape[0]
    for chip in range(chips):
        base = CORES * part * chip
        for ref, side in ((mine_ref, core), (other_ref, 1 - core)):
            out_ref[index, pl.ds(pl.multiple_of(base + part * side, part), part), :] = ref[chip, share * part:(share + 1) * part, :]


def emit_rows(result_ref, core, part, keep_ref, send_ref):
    step, grad = pl.program_id(1), pl.program_id(0)
    for local in range(ROWS // (CORES * part)):
        chip = step * (ROWS // (CORES * part)) + local
        spot = pl.ds(pl.multiple_of(grad * part, part), part)
        for ref, side in ((keep_ref, core), (send_ref, 1 - core)):
            ref[chip, spot, :] = result_ref[pl.ds(pl.multiple_of(local * CORES * part + part * side, part), part), :]


def first_kernel(place_ref, grad_ref, sketch_ref, keep_ref, send_ref, high_ref, low_ref, result_ref):
    part = keep_ref.shape[1] // pl.num_programs(0)

    @pl.when((pl.program_id(0) == 0) & (pl.program_id(1) == 0))
    def _():
        high_ref[...], low_ref[...] = split(sketch_ref[...])

    result_ref[...] = triple(split(grad_ref[0]), (high_ref[...], low_ref[...]), NEAR)
    emit_rows(result_ref, place_ref[0], keep_ref.shape[1] // 2, keep_ref, send_ref)


def first_product(place, gradients, sketch, chips, part):
    grads, depth, width = gradients.shape
    rank = sketch.shape[1]
    shape = (chips, grads * part, rank)
    return pl.pallas_call(
        first_kernel,
        grid=(grads, depth // ROWS),
        in_specs=[SMEM, pl.BlockSpec((1, ROWS, width), lambda g, m: (g, m, 0)), full_block(sketch.shape)],
        out_specs=[full_block(shape)] * 2,
        out_shape=[jax.ShapeDtypeStruct(shape, jnp.float32)] * 2,
        scratch_shapes=[pltpu.VMEM((width, rank), jnp.bfloat16)] * 2 + [pltpu.VMEM((ROWS, rank), jnp.float32)],
        compiler_params=params(2),
    )(place, gradients, sketch)


def emit_quarter(order_ref, grad_ref, high_ref, low_ref, out_refs, left_high, left_low):
    quarter = pl.program_id(0)
    grad = quarter // 2
    slots = order_ref.shape[1]
    for slot in range(slots):
        source = pl.ds(pl.multiple_of(order_ref[quarter, slot] * BLOCK, BLOCK), BLOCK)
        left_high[slot * BLOCK:(slot + 1) * BLOCK, :] = high_ref[grad, source, :]
        left_low[slot * BLOCK:(slot + 1) * BLOCK, :] = low_ref[grad, source, :]
    right = split(grad_ref[0])
    half = slots * BLOCK // 2
    for number in range(len(out_refs) // 2):

        @pl.when(quarter == number)
        def _():
            for side in range(2):
                part = slice(side * half, (side + 1) * half)
                out_refs[2 * number + side][...] = triple((left_high[part, :], left_low[part, :]), right, NEAR)


def pull_kernel(place_ref, order_ref, grad_ref, mine_ref, other_ref, *refs):
    out_refs, (high_ref, low_ref, left_high, left_low, whole_ref) = refs[:-5], refs[-5:]
    grads, _, _ = high_ref.shape

    @pl.when(pl.program_id(0) == 0)
    def _():
        for g in range(grads):
            place_rows(whole_ref, g, mine_ref.shape[1] // grads, g, place_ref[0], mine_ref, other_ref)
            high_ref[g], low_ref[g] = split(whole_ref[g].T)

    emit_quarter(order_ref, grad_ref, high_ref, low_ref, out_refs, left_high, left_low)


def quarter_shapes(gradients, rank):
    grads, depth, width = gradients.shape
    shape = (rank // 2, width // 2)
    scratch = [pltpu.VMEM((grads, rank, depth), jnp.bfloat16)] * 2 + [pltpu.VMEM((rank, depth), jnp.bfloat16)] * 2
    block = pl.BlockSpec((1, depth, width // 2), lambda q: (q // 2, 0, q % 2))
    return block, [full_block(shape)] * (4 * grads), [jax.ShapeDtypeStruct(shape, jnp.float32)] * (4 * grads), scratch


def pull(place, order, gradients, mine, other):
    grads, depth, width = gradients.shape
    rank = mine.shape[2]
    block, out_specs, out_shape, scratch = quarter_shapes(gradients, rank)
    return pl.pallas_call(
        pull_kernel,
        grid=(2 * grads,),
        in_specs=[SMEM, SMEM, block, full_block(mine.shape), full_block(other.shape)],
        out_specs=out_specs,
        out_shape=out_shape,
        scratch_shapes=scratch + [pltpu.VMEM((grads, depth, rank), jnp.float32)],
        compiler_params=params(1),
    )(place, order, gradients, mine, other)


def second_kernel(place_ref, grad_ref, *refs):
    pieces, (keep_ref, send_ref, high_ref, low_ref, result_ref) = refs[:-5], refs[-5:]
    grads, rank, width = high_ref.shape
    half = width // 2
    part = keep_ref.shape[1] // (grads + 1)
    core = place_ref[0]
    grad = pl.program_id(0)
    for g in range(grads):

        @pl.when((grad == g) & (pl.program_id(1) == 0))
        def _():
            for side in range(2):
                quarter = 2 * g + side
                bit = place_ref[1 + cube_order(quarter)[0]]
                for number, spot in ((0, bit), (1, 1 - bit)):
                    rows = pl.ds(pl.multiple_of(spot * (rank // 2), rank // 2), rank // 2)
                    lanes = slice(side * half, (side + 1) * half)
                    high_ref[g, rows, lanes], low_ref[g, rows, lanes] = split(pieces[2 * quarter + number][...])
            pair = (high_ref[g], low_ref[g])
            gram = triple(pair, pair, FAR).reshape(rank // part, part, rank)

            @pl.when(core == g)
            def _():
                keep_ref[:, grads * part:, :] = gram

            @pl.when(core != g)
            def _():
                send_ref[:, grads * part:, :] = gram

    result_ref[...] = triple(split(grad_ref[0]), (high_ref[grad], low_ref[grad]), FAR)
    emit_rows(result_ref, core, part, keep_ref, send_ref)


def second_product(place, gradients, pieces, chips, part):
    grads, depth, width = gradients.shape
    rank = 2 * pieces[0].shape[0]
    shape = (chips, (grads + 1) * part, rank)
    return pl.pallas_call(
        second_kernel,
        grid=(grads, depth // ROWS),
        in_specs=[SMEM, pl.BlockSpec((1, ROWS, width), lambda g, m: (g, m, 0))] + [full_block(p.shape) for p in pieces],
        out_specs=[full_block(shape)] * 2,
        out_shape=[jax.ShapeDtypeStruct(shape, jnp.float32)] * 2,
        scratch_shapes=[pltpu.VMEM((grads, rank, width), jnp.bfloat16)] * 2 + [pltpu.VMEM((ROWS, rank), jnp.float32)],
        compiler_params=params(2),
    )(place, gradients, *pieces)


def balance_kernel(place_ref, mine_ref, other_ref, out_ref, gram_ref, work_ref, inverse_ref, raw_ref):
    grads, rank, _ = work_ref.shape
    core = place_ref[0]
    chips = mine_ref.shape[0]
    part = rank // chips
    for chip in range(chips):
        work_ref[core, chip * part:(chip + 1) * part, :] = mine_ref[chip, grads * part:, :]
        work_ref[1 - core, chip * part:(chip + 1) * part, :] = other_ref[chip, grads * part:, :]
    for g in range(grads):
        place_rows(raw_ref, g, part, g, core, mine_ref, other_ref)
    invert_factor(work_ref, inverse_ref)
    for g in range(grads):
        out_ref[g] = exact(raw_ref[g], inverse_ref[g], FAR)
    chosen = out_ref[core]
    gram_ref[...] = exact(chosen, chosen, TALL)


def balance(place, mine, other, grads, depth):
    rank = mine.shape[2]
    return pl.pallas_call(
        balance_kernel,
        in_specs=[SMEM, VMEM, VMEM],
        out_specs=[VMEM, VMEM],
        out_shape=[jax.ShapeDtypeStruct((grads, depth, rank), jnp.float32), jax.ShapeDtypeStruct((rank, rank), jnp.float32)],
        scratch_shapes=[pltpu.VMEM((grads, rank, rank), jnp.float32)] * 2 + [pltpu.VMEM((grads, depth, rank), jnp.float32)],
        compiler_params=params(0),
    )(place, mine, other)


def project_kernel(scale, place_ref, order_ref, grad_ref, mine_ref, other_ref, balanced_ref, basis_ref, *refs):
    out_refs, (high_ref, low_ref, left_high, left_low, work_ref, inverse_ref) = refs[:-6], refs[-6:]
    grads, _, _ = high_ref.shape
    part = basis_ref.shape[1]
    core = place_ref[0]

    @pl.when(pl.program_id(0) == 0)
    def _():
        work_ref[core] = mine_ref[...]
        work_ref[1 - core] = other_ref[...]
        invert_factor(work_ref, inverse_ref)
        for g in range(grads):
            high_ref[g], low_ref[g] = split(exact(inverse_ref[g], balanced_ref[g], FAR))
            rows = balanced_ref[g, pl.ds(pl.multiple_of(place_ref[5] * part, part), part), :]
            basis_ref[g] = exact(rows, inverse_ref[g], FAR) * scale

    emit_quarter(order_ref, grad_ref, high_ref, low_ref, out_refs, left_high, left_low)


def project(place, order, gradients, mine, other, balanced, part, scale):
    grads, depth, width = gradients.shape
    rank = balanced.shape[2]
    block, out_specs, out_shape, scratch = quarter_shapes(gradients, rank)
    shape = (grads, part, rank)
    return pl.pallas_call(
        functools.partial(project_kernel, scale),
        grid=(2 * grads,),
        in_specs=[SMEM, SMEM, block, full_block(mine.shape), full_block(other.shape), full_block(balanced.shape)],
        out_specs=[full_block(shape)] + out_specs,
        out_shape=[jax.ShapeDtypeStruct(shape, jnp.float32)] + out_shape,
        scratch_shapes=scratch + [pltpu.VMEM((grads, rank, rank), jnp.float32)] * 2,
        compiler_params=params(1),
    )(place, order, gradients, mine, other, balanced)


def swap_core(value):
    size = lax.axis_size("col")
    return lax.ppermute(value, "col", [(i, i ^ 1) for i in range(size)])


def chips_exchange(value):
    size = lax.axis_size("col")
    groups = [list(range(core, size, CORES)) for core in range(CORES)]
    return lax.all_to_all(value, "col", 0, 0, axis_index_groups=groups, tiled=True)


def spread(value, count):
    return jnp.broadcast_to(value[None], (count,) + value.shape)


def sum_columns(keep, send):
    mine = jnp.sum(chips_exchange(keep + swap_core(send)), 0)
    mine = chips_exchange(spread(mine, keep.shape[0]))
    return (mine, swap_core(mine))


def cube_partner(axis):
    pairs = []
    for y in range(SIDE):
        for x in range(SIDE):
            other = (y, x ^ 1), (y, SIDE - 1 - x), (y ^ 1, x), (SIDE - 1 - y, x)
            pairs.append((SIDE * y + x, SIDE * other[axis][0] + other[axis][1]))
    return pairs


def cube_bits(place):
    bits = []
    for digit in (place % SIDE, place // SIDE):
        bits += [(digit ^ (digit >> 1)) & 1, digit >> 1]
    return bits


def cube_order(quarter):
    return [CUBE[(quarter + step) % len(CUBE)] for step in range(len(CUBE))]


def cube_places(quarter):
    places = [0] * SIDE**2
    for place in range(SIDE**2):
        bits = cube_bits(place)
        position = 0
        for axis in cube_order(quarter):
            position = 2 * position + bits[axis]
        places[position] = place
    return places


def send_first(bits, tables):
    rows = []
    for quarter, table in enumerate(tables):
        low, high = jnp.array(table[:len(table) // 2], jnp.int32), jnp.array(table[len(table) // 2:], jnp.int32)
        bit = bits[cube_order(quarter)[0]]
        rows.append(jnp.concatenate([jnp.where(bit == 0, high, low), jnp.where(bit == 0, low, high)]))
    return jnp.stack(rows)


def scatter_sum(pairs, bits):
    quarters = [None] * len(pairs)
    for step in range(len(CUBE)):
        sent = []
        for q, (away, kept) in enumerate(pairs):
            sent.append(lax.ppermute(away, "row", cube_partner(cube_order(q)[step])))
        for q, (away, kept) in enumerate(pairs):
            quarters[q] = kept + sent[q]
        if step + 1 == len(CUBE):
            return quarters
        for q, value in enumerate(quarters):
            bit = bits[cube_order(q)[step + 1]]
            half = value.shape[0] // 2
            pairs[q] = (lax.dynamic_slice_in_dim(value, (1 - bit) * half, half, 0), lax.dynamic_slice_in_dim(value, bit * half, half, 0))


def gather(quarters, bits):
    for step in reversed(range(len(CUBE))):
        got = [lax.ppermute(value, "row", cube_partner(cube_order(q)[step])) for q, value in enumerate(quarters)]
        if step == 0:
            return [piece for q in range(len(quarters)) for piece in (quarters[q], got[q])]
        for q, value in enumerate(quarters):
            high = bits[cube_order(q)[step]] == 1
            quarters[q] = jnp.concatenate([jnp.where(high, got[q], value), jnp.where(high, value, got[q])], 0)


def shards(gradients, sketch):
    grads, depth, width = gradients.shape
    rank = sketch.shape[1]
    row_size, col_size = lax.axis_size("row"), lax.axis_size("col")
    chip_count = col_size // CORES
    part = depth // col_size
    total_rows = depth * row_size

    bits = cube_bits(lax.axis_index("row"))
    col = lax.axis_index("col")
    place = jnp.stack([col % CORES] + bits + [col]).astype(jnp.int32)
    plain = send_first(bits, [list(range(row_size))] * (2 * grads))
    final = send_first(bits, [cube_places(q) for q in range(2 * grads)])

    mine, other = sum_columns(*first_product(place, gradients, sketch, chip_count, part))
    outs = pull(place, plain, gradients, mine, other)
    quarters = scatter_sum([(outs[2 * q], outs[2 * q + 1]) for q in range(2 * grads)], bits)
    pieces = gather(quarters, bits)
    mine, other = sum_columns(*second_product(place, gradients, pieces, chip_count, part))

    balanced, gram_part = balance(place, mine, other, grads, depth)
    gram_mine = jnp.sum(lax.all_to_all(gram_part.reshape(row_size, rank // row_size, rank), "row", 0, 0, tiled=True), 0)
    gram = lax.all_to_all(spread(gram_mine, row_size), "row", 0, 0, tiled=True).reshape(rank, rank)

    basis, *outs = project(place, final, gradients, gram, swap_core(gram), balanced, part, float(total_rows) ** 0.5)
    quarters = scatter_sum([(outs[2 * q], outs[2 * q + 1]) for q in range(2 * grads)], bits)
    projected = jnp.stack([jnp.concatenate(quarters[2 * g:2 * g + 2], 1) for g in range(grads)])
    return (basis, projected)


def solution(mesh):
    in_specs = (P(None, "row", "col"), P("col", None))
    out_specs = (P(None, ("row", "col"), None), P(None, "row", "col"))
    return jax.shard_map(shards, mesh=mesh, in_specs=in_specs, out_specs=out_specs, check_vma=False)
```

```python
import functools

import jax
import jax.numpy as jnp
from jax import lax
from jax.experimental import pallas as pl
from jax.experimental.pallas import tpu as pltpu
from jax.sharding import PartitionSpec as P

FULL = lax.Precision.HIGHEST
CORES = 2
PANEL = 32
GROUP = 8
LANES = 128
SIDE = 4
ORDERS = ((0, 1, 2, 3), (1, 0, 2, 3), (2, 3, 0, 1), (3, 2, 0, 1))
BLOCK = 16
ROWS = 512
NEAR = (((1,), (0,)), ((), ()))
FAR = (((1,), (1,)), ((), ()))
TALL = (((0,), (0,)), ((), ()))
SMEM = pl.BlockSpec(memory_space=pltpu.SMEM)
VMEM = pl.BlockSpec(memory_space=pltpu.VMEM)


def split(value):
    high = value.astype(jnp.bfloat16)
    return (high, (value - high.astype(jnp.float32)).astype(jnp.bfloat16))


def triple(left, right, dims):
    def dot(a, b):
        return lax.dot_general(a, b, dims, preferred_element_type=jnp.float32)

    return dot(left[0], right[0]) + dot(left[0], right[1]) + dot(left[1], right[0])


def exact(left, right, dims):
    return lax.dot_general(left, right, dims, precision=FULL, preferred_element_type=jnp.float32)


def full_block(shape):
    return pl.BlockSpec(shape, lambda *_: (0,) * len(shape))


def params(grid):
    return pltpu.CompilerParams(dimension_semantics=("arbitrary",) * grid, vmem_limit_bytes=28 * 2**20)


def invert_factor(work_ref, out_ref):
    grads, rank, _ = work_ref.shape
    rows = lax.broadcasted_iota(jnp.int32, (PANEL, LANES), 0)
    lanes = lax.broadcasted_iota(jnp.int32, (PANEL, LANES), 1)

    def fill(value):
        return jnp.broadcast_to(value, (PANEL, LANES))

    for lo in range(0, rank, PANEL):
        hi = lo + PANEL
        tile, offset = lo // LANES, lo % LANES
        left = [[work_ref[g, lo:hi, i:i + LANES] for i in range(0, rank, LANES)] for g in range(grads)]
        right = [jnp.where(lanes == rows + offset, 1.0, 0.0) for g in range(grads)]
        for start in range(0, PANEL, GROUP):
            columns = [[fill(left[g][tile][:, offset + start + j:offset + start + j + 1]) for j in range(GROUP)] for g in range(grads)]
            for j in range(GROUP):
                k = start + j
                for g in range(grads):
                    inverse = lax.rsqrt(fill(columns[g][j][k:k + 1, :]))
                    factor = columns[g][j] * inverse
                    for i in range(j + 1, GROUP):
                        columns[g][i] = columns[g][i] - factor * fill(factor[start + i:start + i + 1, :])

                    def eliminate(value):
                        pivot = fill(value[k:k + 1, :]) * inverse
                        return jnp.where(rows > k, value - factor * pivot, jnp.where(rows == k, pivot, value))

                    left[g] = [eliminate(value) for value in left[g]]
                    right[g] = eliminate(right[g])
        inside = (lanes >= offset) & (lanes < offset + PANEL)
        for g in range(grads):
            whole = [jnp.where(inside, right[g], value) if i == tile else value for i, value in enumerate(left[g])]
            for i, value in enumerate(whole):
                known = jnp.where(lanes + i * LANES < hi, value, 0.0)
                out_ref[g, lo:hi, i * LANES:(i + 1) * LANES] = known
            if hi < rank:
                skip = hi // LANES
                update = exact(jnp.concatenate(left[g][skip:], 1), jnp.concatenate(whole, 1), TALL)
                places = lax.broadcasted_iota(jnp.int32, (rank - hi, rank), 1)
                kept = jnp.where((places >= lo) & (places < hi), 0.0, work_ref[g, hi:, :])
                work_ref[g, hi:, :] = kept - update[hi - skip * LANES:]


def place_rows(out_ref, index, part, share, core, mine_ref, other_ref):
    chips = mine_ref.shape[0]
    for chip in range(chips):
        base = CORES * part * chip
        for ref, side in ((mine_ref, core), (other_ref, 1 - core)):
            out_ref[index, pl.ds(pl.multiple_of(base + part * side, part), part), :] = ref[chip, share * part:(share + 1) * part, :]


def emit_rows(result_ref, core, part, keep_ref, send_ref):
    step, grad = pl.program_id(1), pl.program_id(0)
    for local in range(ROWS // (CORES * part)):
        chip = step * (ROWS // (CORES * part)) + local
        spot = pl.ds(pl.multiple_of(grad * part, part), part)
        for ref, side in ((keep_ref, core), (send_ref, 1 - core)):
            ref[chip, spot, :] = result_ref[pl.ds(pl.multiple_of(local * CORES * part + part * side, part), part), :]


def first_kernel(place_ref, grad_ref, sketch_ref, keep_ref, send_ref, high_ref, low_ref, result_ref):
    part = keep_ref.shape[1] // pl.num_programs(0)

    @pl.when((pl.program_id(0) == 0) & (pl.program_id(1) == 0))
    def _():
        high_ref[...], low_ref[...] = split(sketch_ref[...])

    result_ref[...] = triple(split(grad_ref[0]), (high_ref[...], low_ref[...]), NEAR)
    emit_rows(result_ref, place_ref[0], keep_ref.shape[1] // 2, keep_ref, send_ref)


def first_product(place, gradients, sketch, chips, part):
    grads, depth, width = gradients.shape
    rank = sketch.shape[1]
    shape = (chips, grads * part, rank)
    return pl.pallas_call(
        first_kernel,
        grid=(grads, depth // ROWS),
        in_specs=[SMEM, pl.BlockSpec((1, ROWS, width), lambda g, m: (g, m, 0)), full_block(sketch.shape)],
        out_specs=[full_block(shape)] * 2,
        out_shape=[jax.ShapeDtypeStruct(shape, jnp.float32)] * 2,
        scratch_shapes=[pltpu.VMEM((width, rank), jnp.bfloat16)] * 2 + [pltpu.VMEM((ROWS, rank), jnp.float32)],
        compiler_params=params(2),
    )(place, gradients, sketch)


def emit_quarter(order_ref, grad_ref, high_ref, low_ref, out_refs, left_high, left_low):
    quarter = pl.program_id(0)
    grad = quarter // 2
    slots = order_ref.shape[1]
    for slot in range(slots):
        source = pl.ds(pl.multiple_of(order_ref[quarter, slot] * BLOCK, BLOCK), BLOCK)
        left_high[slot * BLOCK:(slot + 1) * BLOCK, :] = high_ref[grad, source, :]
        left_low[slot * BLOCK:(slot + 1) * BLOCK, :] = low_ref[grad, source, :]
    rh, rl = split(grad_ref[0])
    lh, ll = left_high[...], left_low[...]
    both = lax.dot_general(jnp.concatenate([lh, ll], 0), rh, NEAR, preferred_element_type=jnp.float32)
    result = both[:lh.shape[0]] + both[lh.shape[0]:] + lax.dot_general(lh, rl, NEAR, preferred_element_type=jnp.float32)
    half = slots * BLOCK // 2
    for number in range(len(out_refs) // 2):

        @pl.when(quarter == number)
        def _():
            for side in range(2):
                out_refs[2 * number + side][...] = result[side * half:(side + 1) * half]


def pull_kernel(place_ref, order_ref, grad_ref, mine_ref, other_ref, *refs):
    out_refs, (high_ref, low_ref, left_high, left_low, whole_ref) = refs[:-5], refs[-5:]
    grads, _, _ = high_ref.shape

    @pl.when(pl.program_id(0) == 0)
    def _():
        for g in range(grads):
            place_rows(whole_ref, g, mine_ref.shape[1] // grads, g, place_ref[0], mine_ref, other_ref)
            high_ref[g], low_ref[g] = split(whole_ref[g].T)

    emit_quarter(order_ref, grad_ref, high_ref, low_ref, out_refs, left_high, left_low)


def quarter_shapes(gradients, rank):
    grads, depth, width = gradients.shape
    shape = (rank // 2, width // 2)
    scratch = [pltpu.VMEM((grads, rank, depth), jnp.bfloat16)] * 2 + [pltpu.VMEM((rank, depth), jnp.bfloat16)] * 2
    block = pl.BlockSpec((1, depth, width // 2), lambda q: (q // 2, 0, q % 2))
    return block, [full_block(shape)] * (4 * grads), [jax.ShapeDtypeStruct(shape, jnp.float32)] * (4 * grads), scratch


def pull(place, order, gradients, mine, other):
    grads, depth, width = gradients.shape
    rank = mine.shape[2]
    block, out_specs, out_shape, scratch = quarter_shapes(gradients, rank)
    return pl.pallas_call(
        pull_kernel,
        grid=(2 * grads,),
        in_specs=[SMEM, SMEM, block, full_block(mine.shape), full_block(other.shape)],
        out_specs=out_specs,
        out_shape=out_shape,
        scratch_shapes=scratch + [pltpu.VMEM((grads, depth, rank), jnp.float32)],
        compiler_params=params(1),
    )(place, order, gradients, mine, other)


def second_kernel(place_ref, grad_ref, *refs):
    pieces, (keep_ref, send_ref, pulled_ref, high_ref, low_ref, result_ref) = refs[:-6], refs[-6:]
    rank, width = pulled_ref.shape
    grads = len(pieces) // 4
    half = width // 2
    part = keep_ref.shape[1] // (grads + 1)
    core = place_ref[0]
    grad = pl.program_id(0)
    for g in range(grads):

        @pl.when((grad == g) & (pl.program_id(1) == 0))
        def _():
            for side in range(2):
                quarter = 2 * g + side
                bit = place_ref[1 + cube_order(quarter)[0]]
                for number, spot in ((0, bit), (1, 1 - bit)):
                    rows = pl.ds(pl.multiple_of(spot * (rank // 2), rank // 2), rank // 2)
                    lanes = slice(side * half, (side + 1) * half)
                    pulled_ref[rows, lanes] = pieces[2 * quarter + number][...]
            high, low = split(pulled_ref[...].T)
            high_ref[...], low_ref[...] = high, low
            gram = triple(split(pulled_ref[...]), (high, low), NEAR).reshape(rank // part, part, rank)

            @pl.when(core == g)
            def _():
                keep_ref[:, grads * part:, :] = gram

            @pl.when(core != g)
            def _():
                send_ref[:, grads * part:, :] = gram

    result_ref[...] = triple(split(grad_ref[0]), (high_ref[...], low_ref[...]), NEAR)
    emit_rows(result_ref, core, part, keep_ref, send_ref)


def second_product(place, gradients, pieces, chips, part):
    grads, depth, width = gradients.shape
    rank = 2 * pieces[0].shape[0]
    shape = (chips, (grads + 1) * part, rank)
    return pl.pallas_call(
        second_kernel,
        grid=(grads, depth // ROWS),
        in_specs=[SMEM, pl.BlockSpec((1, ROWS, width), lambda g, m: (g, m, 0))] + [full_block(p.shape) for p in pieces],
        out_specs=[full_block(shape)] * 2,
        out_shape=[jax.ShapeDtypeStruct(shape, jnp.float32)] * 2,
        scratch_shapes=[pltpu.VMEM((rank, width), jnp.float32)] + [pltpu.VMEM((width, rank), jnp.bfloat16)] * 2 + [pltpu.VMEM((ROWS, rank), jnp.float32)],
        compiler_params=params(2),
    )(place, gradients, *pieces)


def balance_kernel(place_ref, mine_ref, other_ref, out_ref, gram_ref, work_ref, inverse_ref, raw_ref):
    grads, rank, _ = work_ref.shape
    core = place_ref[0]
    chips = mine_ref.shape[0]
    part = rank // chips
    for chip in range(chips):
        work_ref[core, chip * part:(chip + 1) * part, :] = mine_ref[chip, grads * part:, :]
        work_ref[1 - core, chip * part:(chip + 1) * part, :] = other_ref[chip, grads * part:, :]
    for g in range(grads):
        place_rows(raw_ref, g, part, g, core, mine_ref, other_ref)
    invert_factor(work_ref, inverse_ref)
    for g in range(grads):
        out_ref[g] = exact(raw_ref[g], inverse_ref[g], FAR)
    chosen = out_ref[core]
    gram_ref[...] = exact(chosen, chosen, TALL)


def balance(place, mine, other, grads, depth):
    rank = mine.shape[2]
    return pl.pallas_call(
        balance_kernel,
        in_specs=[SMEM, VMEM, VMEM],
        out_specs=[VMEM, VMEM],
        out_shape=[jax.ShapeDtypeStruct((grads, depth, rank), jnp.float32), jax.ShapeDtypeStruct((rank, rank), jnp.float32)],
        scratch_shapes=[pltpu.VMEM((grads, rank, rank), jnp.float32)] * 2 + [pltpu.VMEM((grads, depth, rank), jnp.float32)],
        compiler_params=params(0),
    )(place, mine, other)


def project_kernel(scale, place_ref, order_ref, grad_ref, mine_ref, other_ref, balanced_ref, basis_ref, *refs):
    out_refs, (high_ref, low_ref, left_high, left_low, work_ref, inverse_ref) = refs[:-6], refs[-6:]
    grads, _, _ = high_ref.shape
    part = basis_ref.shape[1]
    core = place_ref[0]

    @pl.when(pl.program_id(0) == 0)
    def _():
        work_ref[core] = mine_ref[...]
        work_ref[1 - core] = other_ref[...]
        invert_factor(work_ref, inverse_ref)
        for g in range(grads):
            high_ref[g], low_ref[g] = split(exact(inverse_ref[g], balanced_ref[g], FAR))
            rows = balanced_ref[g, pl.ds(pl.multiple_of(place_ref[5] * part, part), part), :]
            basis_ref[g] = exact(rows, inverse_ref[g], FAR) * scale

    emit_quarter(order_ref, grad_ref, high_ref, low_ref, out_refs, left_high, left_low)


def project(place, order, gradients, mine, other, balanced, part, scale):
    grads, depth, width = gradients.shape
    rank = balanced.shape[2]
    block, out_specs, out_shape, scratch = quarter_shapes(gradients, rank)
    shape = (grads, part, rank)
    return pl.pallas_call(
        functools.partial(project_kernel, scale),
        grid=(2 * grads,),
        in_specs=[SMEM, SMEM, block, full_block(mine.shape), full_block(other.shape), full_block(balanced.shape)],
        out_specs=[full_block(shape)] + out_specs,
        out_shape=[jax.ShapeDtypeStruct(shape, jnp.float32)] + out_shape,
        scratch_shapes=scratch + [pltpu.VMEM((grads, rank, rank), jnp.float32)] * 2,
        compiler_params=params(1),
    )(place, order, gradients, mine, other, balanced)


def swap_core(value):
    size = lax.axis_size("col")
    return lax.ppermute(value, "col", [(i, i ^ 1) for i in range(size)])


def chips_exchange(value):
    size = lax.axis_size("col")
    groups = [list(range(core, size, CORES)) for core in range(CORES)]
    return lax.all_to_all(value, "col", 0, 0, axis_index_groups=groups, tiled=True)


def spread(value, count):
    return jnp.broadcast_to(value[None], (count,) + value.shape)


def sum_columns(keep, send):
    mine = jnp.sum(chips_exchange(keep + swap_core(send)), 0)
    mine = chips_exchange(spread(mine, keep.shape[0]))
    return (mine, swap_core(mine))


def cube_partner(axis):
    pairs = []
    for y in range(SIDE):
        for x in range(SIDE):
            other = (y, x ^ 1), (y, SIDE - 1 - x), (y ^ 1, x), (SIDE - 1 - y, x)
            pairs.append((SIDE * y + x, SIDE * other[axis][0] + other[axis][1]))
    return pairs


def cube_bits(place):
    bits = []
    for digit in (place % SIDE, place // SIDE):
        bits += [(digit ^ (digit >> 1)) & 1, digit >> 1]
    return bits


def cube_order(quarter):
    return ORDERS[quarter % len(ORDERS)]


def cube_places(quarter):
    places = [0] * SIDE**2
    for place in range(SIDE**2):
        bits = cube_bits(place)
        position = 0
        for axis in cube_order(quarter):
            position = 2 * position + bits[axis]
        places[position] = place
    return places


def send_first(bits, tables):
    rows = []
    for quarter, table in enumerate(tables):
        low, high = jnp.array(table[:len(table) // 2], jnp.int32), jnp.array(table[len(table) // 2:], jnp.int32)
        bit = bits[cube_order(quarter)[0]]
        rows.append(jnp.concatenate([jnp.where(bit == 0, high, low), jnp.where(bit == 0, low, high)]))
    return jnp.stack(rows)


def across(value, quarter, step):
    return lax.ppermute(value, "row", cube_partner(cube_order(quarter)[step]))


def halves(value, bit):
    half = value.shape[0] // 2
    return (lax.dynamic_slice_in_dim(value, (1 - bit) * half, half, 0), lax.dynamic_slice_in_dim(value, bit * half, half, 0))


def scatter_sum(pairs, bits):
    numbers = list(range(len(pairs)))
    for step in range(4):
        sent = [across(away, q, step) for q, (away, kept) in zip(numbers, pairs)]
        values = [kept + got for got, (away, kept) in zip(sent, pairs)]
        if step == 3:
            return values
        if step == 1:
            numbers = numbers[::2]
            values = [jnp.concatenate(values[q:q + 2], 1) for q in numbers]
        pairs = [halves(value, bits[cube_order(q)[step + 1]]) for q, value in zip(numbers, values)]


def gather(values, bits):
    numbers = list(range(0, 2 * len(values), 2))
    for step in (3, 2, 1, 0):
        got = [across(value, q, step) for q, value in zip(numbers, values)]
        if step == 0:
            return [piece for pair in zip(values, got) for piece in pair]
        wide = []
        for q, value, other in zip(numbers, values, got):
            high = bits[cube_order(q)[step]] == 1
            wide.append(jnp.concatenate([jnp.where(high, other, value), jnp.where(high, value, other)], 0))
        values = wide
        if step == 2:
            numbers = [number for q in numbers for number in (q, q + 1)]
            values = [piece for value in wide for piece in jnp.split(value, 2, 1)]


def shards(gradients, sketch):
    grads, depth, width = gradients.shape
    rank = sketch.shape[1]
    row_size, col_size = lax.axis_size("row"), lax.axis_size("col")
    chip_count = col_size // CORES
    part = depth // col_size
    total_rows = depth * row_size

    bits = cube_bits(lax.axis_index("row"))
    col = lax.axis_index("col")
    place = jnp.stack([col % CORES] + bits + [col]).astype(jnp.int32)
    plain = send_first(bits, [list(range(row_size))] * (2 * grads))
    final = send_first(bits, [cube_places(q) for q in range(2 * grads)])

    mine, other = sum_columns(*first_product(place, gradients, sketch, chip_count, part))
    outs = pull(place, plain, gradients, mine, other)
    quarters = scatter_sum([(outs[2 * q], outs[2 * q + 1]) for q in range(2 * grads)], bits)
    pieces = gather(quarters, bits)
    mine, other = sum_columns(*second_product(place, gradients, pieces, chip_count, part))

    balanced, gram_part = balance(place, mine, other, grads, depth)
    gram_mine = jnp.sum(lax.all_to_all(gram_part.reshape(row_size, rank // row_size, rank), "row", 0, 0, tiled=True), 0)
    gram = lax.all_to_all(spread(gram_mine, row_size), "row", 0, 0, tiled=True).reshape(rank, rank)

    basis, *outs = project(place, final, gradients, gram, swap_core(gram), balanced, part, float(total_rows) ** 0.5)
    quarters = scatter_sum([(outs[2 * q], outs[2 * q + 1]) for q in range(2 * grads)], bits)
    return (basis, jnp.stack(quarters))


def solution(mesh):
    in_specs = (P(None, "row", "col"), P("col", None))
    out_specs = (P(None, ("row", "col"), None), P(None, "row", "col"))
    return jax.shard_map(shards, mesh=mesh, in_specs=in_specs, out_specs=out_specs, check_vma=False)
```

```python
import functools

import jax
import jax.numpy as jnp
from jax import lax
from jax.experimental import pallas as pl
from jax.experimental.pallas import tpu as pltpu
from jax.sharding import PartitionSpec as P

FULL = lax.Precision.HIGHEST
CORES = 2
PANEL = 32
GROUP = 8
LANES = 128
SIDE = 4
ORDERS = ((0, 1, 2, 3), (1, 0, 2, 3), (2, 3, 0, 1), (3, 2, 0, 1))
BLOCK = 16
ROWS = 512
NEAR = (((1,), (0,)), ((), ()))
FAR = (((1,), (1,)), ((), ()))
TALL = (((0,), (0,)), ((), ()))
SMEM = pl.BlockSpec(memory_space=pltpu.SMEM)
VMEM = pl.BlockSpec(memory_space=pltpu.VMEM)


def split(value):
    high = value.astype(jnp.bfloat16)
    return (high, (value - high.astype(jnp.float32)).astype(jnp.bfloat16))


def triple(left, right, dims):
    def dot(a, b):
        return lax.dot_general(a, b, dims, preferred_element_type=jnp.float32)

    return dot(left[0], right[0]) + dot(left[0], right[1]) + dot(left[1], right[0])


def exact(left, right, dims):
    return lax.dot_general(left, right, dims, precision=FULL, preferred_element_type=jnp.float32)


def full_block(shape):
    return pl.BlockSpec(shape, lambda *_: (0,) * len(shape))


def params(grid):
    return pltpu.CompilerParams(dimension_semantics=("arbitrary",) * grid, vmem_limit_bytes=48 * 2**20)


def invert_factor(work_ref, out_ref):
    grads, rank, _ = work_ref.shape
    rows = lax.broadcasted_iota(jnp.int32, (PANEL, LANES), 0)
    lanes = lax.broadcasted_iota(jnp.int32, (PANEL, LANES), 1)

    def fill(value):
        return jnp.broadcast_to(value, (PANEL, LANES))

    for lo in range(0, rank, PANEL):
        hi = lo + PANEL
        tile, offset = lo // LANES, lo % LANES
        left = [[work_ref[g, lo:hi, i:i + LANES] for i in range(0, rank, LANES)] for g in range(grads)]
        right = [jnp.where(lanes == rows + offset, 1.0, 0.0) for g in range(grads)]
        for start in range(0, PANEL, GROUP):
            columns = [[fill(left[g][tile][:, offset + start + j:offset + start + j + 1]) for j in range(GROUP)] for g in range(grads)]
            for j in range(GROUP):
                k = start + j
                for g in range(grads):
                    inverse = lax.rsqrt(fill(columns[g][j][k:k + 1, :]))
                    factor = columns[g][j] * inverse
                    for i in range(j + 1, GROUP):
                        columns[g][i] = columns[g][i] - factor * fill(factor[start + i:start + i + 1, :])

                    def eliminate(value):
                        pivot = fill(value[k:k + 1, :]) * inverse
                        return jnp.where(rows > k, value - factor * pivot, jnp.where(rows == k, pivot, value))

                    left[g] = [eliminate(value) for value in left[g]]
                    right[g] = eliminate(right[g])
        inside = (lanes >= offset) & (lanes < offset + PANEL)
        for g in range(grads):
            whole = [jnp.where(inside, right[g], value) if i == tile else value for i, value in enumerate(left[g])]
            for i, value in enumerate(whole):
                known = jnp.where(lanes + i * LANES < hi, value, 0.0)
                out_ref[g, lo:hi, i * LANES:(i + 1) * LANES] = known
            if hi < rank:
                skip = hi // LANES
                update = exact(jnp.concatenate(left[g][skip:], 1), jnp.concatenate(whole, 1), TALL)
                places = lax.broadcasted_iota(jnp.int32, (rank - hi, rank), 1)
                kept = jnp.where((places >= lo) & (places < hi), 0.0, work_ref[g, hi:, :])
                work_ref[g, hi:, :] = kept - update[hi - skip * LANES:]


def place_rows(out_ref, index, part, share, core, mine_ref, other_ref):
    chips = mine_ref.shape[0]
    for chip in range(chips):
        base = CORES * part * chip
        for ref, side in ((mine_ref, core), (other_ref, 1 - core)):
            out_ref[index, pl.ds(pl.multiple_of(base + part * side, part), part), :] = ref[chip, share * part:(share + 1) * part, :]


def emit_rows(result_ref, core, part, keep_ref, send_ref):
    step, grad = pl.program_id(1), pl.program_id(0)
    for local in range(ROWS // (CORES * part)):
        chip = step * (ROWS // (CORES * part)) + local
        spot = pl.ds(pl.multiple_of(grad * part, part), part)
        for ref, side in ((keep_ref, core), (send_ref, 1 - core)):
            ref[chip, spot, :] = result_ref[pl.ds(pl.multiple_of(local * CORES * part + part * side, part), part), :]


def first_kernel(place_ref, grad_ref, sketch_ref, keep_ref, send_ref, high_ref, low_ref, result_ref):
    part = keep_ref.shape[1] // pl.num_programs(0)

    @pl.when((pl.program_id(0) == 0) & (pl.program_id(1) == 0))
    def _():
        high_ref[...], low_ref[...] = split(sketch_ref[...])

    result_ref[...] = triple(split(grad_ref[0]), (high_ref[...], low_ref[...]), NEAR)
    emit_rows(result_ref, place_ref[0], keep_ref.shape[1] // 2, keep_ref, send_ref)


def first_product(place, gradients, sketch, chips, part):
    grads, depth, width = gradients.shape
    rank = sketch.shape[1]
    shape = (chips, grads * part, rank)
    return pl.pallas_call(
        first_kernel,
        grid=(grads, depth // ROWS),
        in_specs=[SMEM, pl.BlockSpec((1, ROWS, width), lambda g, m: (g, m, 0)), full_block(sketch.shape)],
        out_specs=[full_block(shape)] * 2,
        out_shape=[jax.ShapeDtypeStruct(shape, jnp.float32)] * 2,
        scratch_shapes=[pltpu.VMEM((width, rank), jnp.bfloat16)] * 2 + [pltpu.VMEM((ROWS, rank), jnp.float32)],
        compiler_params=params(2),
    )(place, gradients, sketch)


def emit_quarter(order_ref, grad_ref, high_ref, low_ref, out_refs, left_high, left_low):
    quarter = pl.program_id(0)
    grad = quarter // 2
    slots = order_ref.shape[1]
    for slot in range(slots):
        source = pl.ds(pl.multiple_of(order_ref[quarter, slot] * BLOCK, BLOCK), BLOCK)
        left_high[slot * BLOCK:(slot + 1) * BLOCK, :] = high_ref[grad, source, :]
        left_low[slot * BLOCK:(slot + 1) * BLOCK, :] = low_ref[grad, source, :]
    rh, rl = split(grad_ref[0])
    lh, ll = left_high[...], left_low[...]
    both = lax.dot_general(jnp.concatenate([lh, ll], 0), rh, NEAR, preferred_element_type=jnp.float32)
    result = both[:lh.shape[0]] + both[lh.shape[0]:] + lax.dot_general(lh, rl, NEAR, preferred_element_type=jnp.float32)
    half = slots * BLOCK // 2
    for number in range(len(out_refs) // 2):

        @pl.when(quarter == number)
        def _():
            for side in range(2):
                out_refs[2 * number + side][...] = result[side * half:(side + 1) * half]


def pull_kernel(place_ref, order_ref, grad_ref, mine_ref, other_ref, *refs):
    out_refs, (high_ref, low_ref, left_high, left_low, whole_ref) = refs[:-5], refs[-5:]
    grads, _, _ = high_ref.shape

    @pl.when(pl.program_id(0) == 0)
    def _():
        for g in range(grads):
            place_rows(whole_ref, g, mine_ref.shape[1] // grads, g, place_ref[0], mine_ref, other_ref)
            high_ref[g], low_ref[g] = split(whole_ref[g].T)

    emit_quarter(order_ref, grad_ref, high_ref, low_ref, out_refs, left_high, left_low)


def quarter_shapes(gradients, rank):
    grads, depth, width = gradients.shape
    shape = (rank // 2, width // 2)
    scratch = [pltpu.VMEM((grads, rank, depth), jnp.bfloat16)] * 2 + [pltpu.VMEM((rank, depth), jnp.bfloat16)] * 2
    block = pl.BlockSpec((1, depth, width // 2), lambda q: (q // 2, 0, q % 2))
    return block, [full_block(shape)] * (4 * grads), [jax.ShapeDtypeStruct(shape, jnp.float32)] * (4 * grads), scratch


def pull(place, order, gradients, mine, other):
    grads, depth, width = gradients.shape
    rank = mine.shape[2]
    block, out_specs, out_shape, scratch = quarter_shapes(gradients, rank)
    return pl.pallas_call(
        pull_kernel,
        grid=(2 * grads,),
        in_specs=[SMEM, SMEM, block, full_block(mine.shape), full_block(other.shape)],
        out_specs=out_specs,
        out_shape=out_shape,
        scratch_shapes=scratch + [pltpu.VMEM((grads, depth, rank), jnp.float32)],
        compiler_params=params(1),
    )(place, order, gradients, mine, other)


def fold(gram):
    half, rank = gram.shape[0] // 2, gram.shape[0]
    middle = half + half // 2
    corner = [gram[half:middle, half:], gram[middle:rank, half:]]
    return jnp.concatenate([gram[:half], jnp.concatenate(corner, 1)], 0)


def unfold(out_ref, index, folded_ref, source):
    _, rank, _ = out_ref.shape
    half = rank // 2
    middle = half + half // 2
    out_ref[index, :half, :] = folded_ref[source, :half, :]
    out_ref[index, half:middle, half:] = folded_ref[source, half:, :half]
    out_ref[index, middle:, half:] = folded_ref[source, half:, half:]


def second_kernel(place_ref, grad_ref, *refs):
    pieces, (keep_ref, send_ref, pulled_ref, high_ref, low_ref, result_ref) = refs[:-6], refs[-6:]
    rank, width = pulled_ref.shape
    grads = len(pieces) // 4
    half = width // 2
    part = grad_ref.shape[1] // (CORES * keep_ref.shape[0])
    core = place_ref[0]
    grad = pl.program_id(0)
    for g in range(grads):

        @pl.when((grad == g) & (pl.program_id(1) == 0))
        def _():
            for side in range(2):
                quarter = 2 * g + side
                bit = place_ref[1 + cube_order(quarter)[0]]
                for number, spot in ((0, bit), (1, 1 - bit)):
                    rows = pl.ds(pl.multiple_of(spot * (rank // 2), rank // 2), rank // 2)
                    lanes = slice(side * half, (side + 1) * half)
                    pulled_ref[rows, lanes] = pieces[2 * quarter + number][...]
            high, low = split(pulled_ref[...].T)
            high_ref[...], low_ref[...] = high, low
            folded = fold(triple(split(pulled_ref[...]), (high, low), NEAR))
            folded = folded.reshape(keep_ref.shape[0], -1, rank)

            @pl.when(core == g)
            def _():
                keep_ref[:, grads * part:, :] = folded

            @pl.when(core != g)
            def _():
                send_ref[:, grads * part:, :] = folded

    result_ref[...] = triple(split(grad_ref[0]), (high_ref[...], low_ref[...]), NEAR)
    emit_rows(result_ref, core, part, keep_ref, send_ref)


def second_product(place, gradients, pieces, chips, part):
    grads, depth, width = gradients.shape
    rank = 2 * pieces[0].shape[0]
    shape = (chips, grads * part + 3 * rank // 4 // chips, rank)
    return pl.pallas_call(
        second_kernel,
        grid=(grads, depth // ROWS),
        in_specs=[SMEM, pl.BlockSpec((1, ROWS, width), lambda g, m: (g, m, 0))] + [full_block(p.shape) for p in pieces],
        out_specs=[full_block(shape)] * 2,
        out_shape=[jax.ShapeDtypeStruct(shape, jnp.float32)] * 2,
        scratch_shapes=[pltpu.VMEM((rank, width), jnp.float32)] + [pltpu.VMEM((width, rank), jnp.bfloat16)] * 2 + [pltpu.VMEM((ROWS, rank), jnp.float32)],
        compiler_params=params(2),
    )(place, gradients, *pieces)


def balance_kernel(place_ref, mine_ref, other_ref, out_ref, gram_ref, work_ref, inverse_ref, raw_ref, folded_ref):
    grads, rank, _ = work_ref.shape
    core = place_ref[0]
    chips = mine_ref.shape[0]
    part = raw_ref.shape[1] // (CORES * chips)
    piece = folded_ref.shape[1] // chips
    for chip in range(chips):
        for side, ref in enumerate((mine_ref, other_ref)):
            folded_ref[side, chip * piece:(chip + 1) * piece, :] = ref[chip, grads * part:, :]
    work_ref[...] = jnp.zeros(work_ref.shape, jnp.float32)
    unfold(work_ref, core, folded_ref, 0)
    unfold(work_ref, 1 - core, folded_ref, 1)
    for g in range(grads):
        place_rows(raw_ref, g, part, g, core, mine_ref, other_ref)
    invert_factor(work_ref, inverse_ref)
    for g in range(grads):
        out_ref[g] = exact(raw_ref[g], inverse_ref[g], FAR)
    chosen = out_ref[core]
    gram_ref[...] = exact(chosen, chosen, TALL)


def balance(place, mine, other, grads, depth):
    rank = mine.shape[2]
    return pl.pallas_call(
        balance_kernel,
        in_specs=[SMEM, VMEM, VMEM],
        out_specs=[VMEM, VMEM],
        out_shape=[jax.ShapeDtypeStruct((grads, depth, rank), jnp.float32), jax.ShapeDtypeStruct((rank, rank), jnp.float32)],
        scratch_shapes=[pltpu.VMEM((grads, rank, rank), jnp.float32)] * 2 + [pltpu.VMEM((grads, depth, rank), jnp.float32), pltpu.VMEM((2, 3 * rank // 4, rank), jnp.float32)],
        compiler_params=params(0),
    )(place, mine, other)


def project_kernel(scale, place_ref, order_ref, grad_ref, mine_ref, other_ref, balanced_ref, basis_ref, *refs):
    out_refs, (high_ref, low_ref, left_high, left_low, work_ref, inverse_ref) = refs[:-6], refs[-6:]
    grads, _, _ = high_ref.shape
    part = basis_ref.shape[1]
    core = place_ref[0]

    @pl.when(pl.program_id(0) == 0)
    def _():
        work_ref[core] = mine_ref[...]
        work_ref[1 - core] = other_ref[...]
        invert_factor(work_ref, inverse_ref)
        for g in range(grads):
            high_ref[g], low_ref[g] = split(exact(inverse_ref[g], balanced_ref[g], FAR))
            rows = balanced_ref[g, pl.ds(pl.multiple_of(place_ref[5] * part, part), part), :]
            basis_ref[g] = exact(rows, inverse_ref[g], FAR) * scale

    emit_quarter(order_ref, grad_ref, high_ref, low_ref, out_refs, left_high, left_low)


def project(place, order, gradients, mine, other, balanced, part, scale):
    grads, depth, width = gradients.shape
    rank = balanced.shape[2]
    block, out_specs, out_shape, scratch = quarter_shapes(gradients, rank)
    shape = (grads, part, rank)
    return pl.pallas_call(
        functools.partial(project_kernel, scale),
        grid=(2 * grads,),
        in_specs=[SMEM, SMEM, block, full_block(mine.shape), full_block(other.shape), full_block(balanced.shape)],
        out_specs=[full_block(shape)] + out_specs,
        out_shape=[jax.ShapeDtypeStruct(shape, jnp.float32)] + out_shape,
        scratch_shapes=scratch + [pltpu.VMEM((grads, rank, rank), jnp.float32)] * 2,
        compiler_params=params(1),
    )(place, order, gradients, mine, other, balanced)


def swap_core(value):
    size = lax.axis_size("col")
    return lax.ppermute(value, "col", [(i, i ^ 1) for i in range(size)])


def chips_exchange(value):
    size = lax.axis_size("col")
    groups = [list(range(core, size, CORES)) for core in range(CORES)]
    return lax.all_to_all(value, "col", 0, 0, axis_index_groups=groups, tiled=True)


def spread(value, count):
    return jnp.broadcast_to(value[None], (count,) + value.shape)


def sum_columns(keep, send):
    mine = jnp.sum(chips_exchange(keep + swap_core(send)), 0)
    mine = chips_exchange(spread(mine, keep.shape[0]))
    return (mine, swap_core(mine))


def cube_partner(axis):
    pairs = []
    for y in range(SIDE):
        for x in range(SIDE):
            other = (y, x ^ 1), (y, SIDE - 1 - x), (y ^ 1, x), (SIDE - 1 - y, x)
            pairs.append((SIDE * y + x, SIDE * other[axis][0] + other[axis][1]))
    return pairs


def cube_bits(place):
    bits = []
    for digit in (place % SIDE, place // SIDE):
        bits += [(digit ^ (digit >> 1)) & 1, digit >> 1]
    return bits


def cube_order(quarter):
    return ORDERS[quarter % len(ORDERS)]


def cube_places(quarter):
    places = [0] * SIDE**2
    for place in range(SIDE**2):
        bits = cube_bits(place)
        position = 0
        for axis in cube_order(quarter):
            position = 2 * position + bits[axis]
        places[position] = place
    return places


def send_first(bits, tables):
    rows = []
    for quarter, table in enumerate(tables):
        low, high = jnp.array(table[:len(table) // 2], jnp.int32), jnp.array(table[len(table) // 2:], jnp.int32)
        bit = bits[cube_order(quarter)[0]]
        rows.append(jnp.concatenate([jnp.where(bit == 0, high, low), jnp.where(bit == 0, low, high)]))
    return jnp.stack(rows)


def across(value, quarter, step):
    return lax.ppermute(value, "row", cube_partner(cube_order(quarter)[step]))


def halves(value, bit):
    half = value.shape[0] // 2
    return (lax.dynamic_slice_in_dim(value, (1 - bit) * half, half, 0), lax.dynamic_slice_in_dim(value, bit * half, half, 0))


def scatter_sum(pairs, bits):
    numbers = list(range(len(pairs)))
    for step in range(4):
        sent = [across(away, q, step) for q, (away, kept) in zip(numbers, pairs)]
        if step == 3:
            return [kept + got for got, (away, kept) in zip(sent, pairs)]
        parts = []
        for q, got, (away, kept) in zip(numbers, sent, pairs):
            bit = bits[cube_order(q)[step + 1 if step != 1 else 2]]
            parts.append([mine + theirs for mine, theirs in zip(halves(kept, bit), halves(got, bit))])
        if step == 1:
            numbers = numbers[::2]
            parts = [[jnp.concatenate(both, 1) for both in zip(parts[q], parts[q + 1])] for q in numbers]
        pairs = parts


def gather(values, bits):
    numbers = list(range(0, 2 * len(values), 2))
    for step in (3, 2, 1, 0):
        got = [across(value, q, step) for q, value in zip(numbers, values)]
        if step == 0:
            return [piece for pair in zip(values, got) for piece in pair]
        wide = []
        for q, value, other in zip(numbers, values, got):
            high = bits[cube_order(q)[step]] == 1
            wide.append(jnp.concatenate([jnp.where(high, other, value), jnp.where(high, value, other)], 0))
        values = wide
        if step == 2:
            numbers = [number for q in numbers for number in (q, q + 1)]
            values = [piece for value in wide for piece in jnp.split(value, 2, 1)]


def shards(gradients, sketch):
    grads, depth, width = gradients.shape
    rank = sketch.shape[1]
    row_size, col_size = lax.axis_size("row"), lax.axis_size("col")
    chip_count = col_size // CORES
    part = depth // col_size
    total_rows = depth * row_size

    bits = cube_bits(lax.axis_index("row"))
    col = lax.axis_index("col")
    place = jnp.stack([col % CORES] + bits + [col]).astype(jnp.int32)
    plain = send_first(bits, [list(range(row_size))] * (2 * grads))
    final = send_first(bits, [cube_places(q) for q in range(2 * grads)])

    mine, other = sum_columns(*first_product(place, gradients, sketch, chip_count, part))
    outs = pull(place, plain, gradients, mine, other)
    quarters = scatter_sum([(outs[2 * q], outs[2 * q + 1]) for q in range(2 * grads)], bits)
    pieces = gather(quarters, bits)
    mine, other = sum_columns(*second_product(place, gradients, pieces, chip_count, part))

    balanced, gram_part = balance(place, mine, other, grads, depth)
    gram_mine = jnp.sum(lax.all_to_all(gram_part.reshape(row_size, rank // row_size, rank), "row", 0, 0, tiled=True), 0)
    gram = lax.all_to_all(spread(gram_mine, row_size), "row", 0, 0, tiled=True).reshape(rank, rank)

    basis, *outs = project(place, final, gradients, gram, swap_core(gram), balanced, part, float(total_rows) ** 0.5)
    quarters = scatter_sum([(outs[2 * q], outs[2 * q + 1]) for q in range(2 * grads)], bits)
    return (basis, jnp.stack(quarters))


def solution(mesh):
    in_specs = (P(None, "row", "col"), P("col", None))
    out_specs = (P(None, ("row", "col"), None), P(None, "row", "col"))
    return jax.shard_map(shards, mesh=mesh, in_specs=in_specs, out_specs=out_specs, check_vma=False)
```

```python
import functools

import jax
import jax.numpy as jnp
from jax import lax
from jax.experimental import pallas as pl
from jax.experimental.pallas import tpu as pltpu
from jax.sharding import PartitionSpec as P

FULL = lax.Precision.HIGHEST
CORES = 2
PANEL = 32
GROUP = 8
LANES = 128
SIDE = 4
ORDERS = ((0, 1, 2, 3), (1, 0, 2, 3), (2, 3, 0, 1), (3, 2, 0, 1))
BLOCK = 16
ROWS = 512
NEAR = (((1,), (0,)), ((), ()))
FAR = (((1,), (1,)), ((), ()))
TALL = (((0,), (0,)), ((), ()))
SMEM = pl.BlockSpec(memory_space=pltpu.SMEM)
VMEM = pl.BlockSpec(memory_space=pltpu.VMEM)


def split(value):
    high = value.astype(jnp.bfloat16)
    return (high, (value - high.astype(jnp.float32)).astype(jnp.bfloat16))


def triple(left, right, dims):
    def dot(a, b):
        return lax.dot_general(a, b, dims, preferred_element_type=jnp.float32)

    return dot(left[0], right[0]) + dot(left[0], right[1]) + dot(left[1], right[0])


def exact(left, right, dims):
    return lax.dot_general(left, right, dims, precision=FULL, preferred_element_type=jnp.float32)


def full_block(shape):
    return pl.BlockSpec(shape, lambda *_: (0,) * len(shape))


def params(grid):
    return pltpu.CompilerParams(dimension_semantics=("arbitrary",) * grid, vmem_limit_bytes=48 * 2**20)


def invert_factor(work_ref, out_ref):
    grads, rank, _ = work_ref.shape
    rows = lax.broadcasted_iota(jnp.int32, (PANEL, LANES), 0)
    lanes = lax.broadcasted_iota(jnp.int32, (PANEL, LANES), 1)

    def fill(value):
        return jnp.broadcast_to(value, (PANEL, LANES))

    for lo in range(0, rank, PANEL):
        hi = lo + PANEL
        tile, offset = lo // LANES, lo % LANES
        left = [[work_ref[g, lo:hi, i:i + LANES] for i in range(0, rank, LANES)] for g in range(grads)]
        right = [jnp.where(lanes == rows + offset, 1.0, 0.0) for g in range(grads)]
        for start in range(0, PANEL, GROUP):
            columns = [[fill(left[g][tile][:, offset + start + j:offset + start + j + 1]) for j in range(GROUP)] for g in range(grads)]
            for j in range(GROUP):
                k = start + j
                for g in range(grads):
                    inverse = lax.rsqrt(fill(columns[g][j][k:k + 1, :]))
                    factor = columns[g][j] * inverse
                    for i in range(j + 1, GROUP):
                        columns[g][i] = columns[g][i] - factor * fill(factor[start + i:start + i + 1, :])

                    def eliminate(value):
                        pivot = fill(value[k:k + 1, :]) * inverse
                        return jnp.where(rows > k, value - factor * pivot, jnp.where(rows == k, pivot, value))

                    left[g] = [eliminate(value) for value in left[g]]
                    right[g] = eliminate(right[g])
        inside = (lanes >= offset) & (lanes < offset + PANEL)
        for g in range(grads):
            whole = [jnp.where(inside, right[g], value) if i == tile else value for i, value in enumerate(left[g])]
            for i, value in enumerate(whole):
                known = jnp.where(lanes + i * LANES < hi, value, 0.0)
                out_ref[g, lo:hi, i * LANES:(i + 1) * LANES] = known
            if hi < rank:
                skip = hi // LANES
                update = exact(jnp.concatenate(left[g][skip:], 1), jnp.concatenate(whole, 1), TALL)
                places = lax.broadcasted_iota(jnp.int32, (rank - hi, rank), 1)
                kept = jnp.where((places >= lo) & (places < hi), 0.0, work_ref[g, hi:, :])
                work_ref[g, hi:, :] = kept - update[hi - skip * LANES:]


def place_rows(out_ref, index, part, share, core, mine_ref, other_ref):
    chips = mine_ref.shape[0]
    for chip in range(chips):
        base = CORES * part * chip
        for ref, side in ((mine_ref, core), (other_ref, 1 - core)):
            out_ref[index, pl.ds(pl.multiple_of(base + part * side, part), part), :] = ref[chip, share * part:(share + 1) * part, :]


def emit_rows(result_ref, core, part, keep_ref, send_ref):
    step, grad = pl.program_id(1), pl.program_id(0)
    for local in range(ROWS // (CORES * part)):
        chip = step * (ROWS // (CORES * part)) + local
        spot = pl.ds(pl.multiple_of(grad * part, part), part)
        for ref, side in ((keep_ref, core), (send_ref, 1 - core)):
            ref[chip, spot, :] = result_ref[pl.ds(pl.multiple_of(local * CORES * part + part * side, part), part), :]


def first_kernel(place_ref, grad_ref, sketch_ref, keep_ref, send_ref, high_ref, low_ref, result_ref):
    part = keep_ref.shape[1] // pl.num_programs(0)

    @pl.when((pl.program_id(0) == 0) & (pl.program_id(1) == 0))
    def _():
        high_ref[...], low_ref[...] = split(sketch_ref[...])

    result_ref[...] = triple(split(grad_ref[0]), (high_ref[...], low_ref[...]), NEAR)
    emit_rows(result_ref, place_ref[0], keep_ref.shape[1] // 2, keep_ref, send_ref)


def first_product(place, gradients, sketch, chips, part):
    grads, depth, width = gradients.shape
    rank = sketch.shape[1]
    shape = (chips, grads * part, rank)
    return pl.pallas_call(
        first_kernel,
        grid=(grads, depth // ROWS),
        in_specs=[SMEM, pl.BlockSpec((1, ROWS, width), lambda g, m: (g, m, 0)), full_block(sketch.shape)],
        out_specs=[full_block(shape)] * 2,
        out_shape=[jax.ShapeDtypeStruct(shape, jnp.float32)] * 2,
        scratch_shapes=[pltpu.VMEM((width, rank), jnp.bfloat16)] * 2 + [pltpu.VMEM((ROWS, rank), jnp.float32)],
        compiler_params=params(2),
    )(place, gradients, sketch)


def emit_quarter(order_ref, grad_ref, high_ref, low_ref, out_refs, left_high, left_low):
    quarter = pl.program_id(0)
    grad = quarter // 2
    slots = order_ref.shape[1]
    for slot in range(slots):
        source = pl.ds(pl.multiple_of(order_ref[quarter, slot] * BLOCK, BLOCK), BLOCK)
        left_high[slot * BLOCK:(slot + 1) * BLOCK, :] = high_ref[grad, source, :]
        left_low[slot * BLOCK:(slot + 1) * BLOCK, :] = low_ref[grad, source, :]
    rh, rl = split(grad_ref[0])
    lh, ll = left_high[...], left_low[...]
    both = lax.dot_general(jnp.concatenate([lh, ll], 0), rh, NEAR, preferred_element_type=jnp.float32)
    result = both[:lh.shape[0]] + both[lh.shape[0]:] + lax.dot_general(lh, rl, NEAR, preferred_element_type=jnp.float32)
    half = slots * BLOCK // 2
    for number in range(len(out_refs) // 2):

        @pl.when(quarter == number)
        def _():
            for side in range(2):
                out_refs[2 * number + side][...] = result[side * half:(side + 1) * half]


def pull_kernel(grad, place_ref, order_ref, grad_ref, mine_ref, other_ref, *refs):
    out_refs, (high_ref, low_ref, left_high, left_low, whole_ref) = refs[:-5], refs[-5:]
    part = whole_ref.shape[1] // (CORES * mine_ref.shape[0])

    @pl.when(pl.program_id(0) == 0)
    def _():
        place_rows(whole_ref, 0, part, grad, place_ref[0], mine_ref, other_ref)
        high_ref[0], low_ref[0] = split(whole_ref[0].T)

    emit_quarter(order_ref, grad_ref, high_ref, low_ref, out_refs, left_high, left_low)


def quarter_shapes(gradients, rank):
    grads, depth, width = gradients.shape
    shape = (rank // 2, width // 2)
    scratch = [pltpu.VMEM((grads, rank, depth), jnp.bfloat16)] * 2 + [pltpu.VMEM((rank, depth), jnp.bfloat16)] * 2
    block = pl.BlockSpec((1, depth, width // 2), lambda q: (q // 2, 0, q % 2))
    return block, [full_block(shape)] * (4 * grads), [jax.ShapeDtypeStruct(shape, jnp.float32)] * (4 * grads), scratch


def pull(place, order, gradients, mine, other, grad):
    _, depth, width = gradients.shape
    rank = mine.shape[2]
    _, out_specs, out_shape, scratch = quarter_shapes(gradients[:1], rank)
    block = pl.BlockSpec((1, depth, width // 2), lambda q: (grad, 0, q))
    return pl.pallas_call(
        functools.partial(pull_kernel, grad),
        grid=(2,),
        in_specs=[SMEM, SMEM, block, full_block(mine.shape), full_block(other.shape)],
        out_specs=out_specs,
        out_shape=out_shape,
        scratch_shapes=scratch + [pltpu.VMEM((1, depth, rank), jnp.float32)],
        compiler_params=params(1),
    )(place, order, gradients, mine, other)


def fold(gram):
    half, rank = gram.shape[0] // 2, gram.shape[0]
    middle = half + half // 2
    corner = [gram[half:middle, half:], gram[middle:rank, half:]]
    return jnp.concatenate([gram[:half], jnp.concatenate(corner, 1)], 0)


def unfold(out_ref, index, folded_ref, source):
    _, rank, _ = out_ref.shape
    half = rank // 2
    middle = half + half // 2
    out_ref[index, :half, :] = folded_ref[source, :half, :]
    out_ref[index, half:middle, half:] = folded_ref[source, half:, :half]
    out_ref[index, middle:, half:] = folded_ref[source, half:, half:]


def second_kernel(place_ref, grad_ref, *refs):
    pieces, (keep_ref, send_ref, pulled_ref, high_ref, low_ref, result_ref) = refs[:-6], refs[-6:]
    rank, width = pulled_ref.shape
    grads = len(pieces) // 4
    half = width // 2
    part = grad_ref.shape[1] // (CORES * keep_ref.shape[0])
    core = place_ref[0]
    grad = pl.program_id(0)
    for g in range(grads):

        @pl.when((grad == g) & (pl.program_id(1) == 0))
        def _():
            for side in range(2):
                quarter = 2 * g + side
                bit = place_ref[1 + cube_order(quarter)[0]]
                for number, spot in ((0, bit), (1, 1 - bit)):
                    rows = pl.ds(pl.multiple_of(spot * (rank // 2), rank // 2), rank // 2)
                    lanes = slice(side * half, (side + 1) * half)
                    pulled_ref[rows, lanes] = pieces[2 * quarter + number][...]
            high, low = split(pulled_ref[...].T)
            high_ref[...], low_ref[...] = high, low
            folded = fold(triple(split(pulled_ref[...]), (high, low), NEAR))
            folded = folded.reshape(keep_ref.shape[0], -1, rank)

            @pl.when(core == g)
            def _():
                keep_ref[:, grads * part:, :] = folded

            @pl.when(core != g)
            def _():
                send_ref[:, grads * part:, :] = folded

    result_ref[...] = triple(split(grad_ref[0]), (high_ref[...], low_ref[...]), NEAR)
    emit_rows(result_ref, core, part, keep_ref, send_ref)


def second_product(place, gradients, pieces, chips, part):
    grads, depth, width = gradients.shape
    rank = 2 * pieces[0].shape[0]
    shape = (chips, grads * part + 3 * rank // 4 // chips, rank)
    return pl.pallas_call(
        second_kernel,
        grid=(grads, depth // ROWS),
        in_specs=[SMEM, pl.BlockSpec((1, ROWS, width), lambda g, m: (g, m, 0))] + [full_block(p.shape) for p in pieces],
        out_specs=[full_block(shape)] * 2,
        out_shape=[jax.ShapeDtypeStruct(shape, jnp.float32)] * 2,
        scratch_shapes=[pltpu.VMEM((rank, width), jnp.float32)] + [pltpu.VMEM((width, rank), jnp.bfloat16)] * 2 + [pltpu.VMEM((ROWS, rank), jnp.float32)],
        compiler_params=params(2),
    )(place, gradients, *pieces)


def balance_kernel(place_ref, mine_ref, other_ref, out_ref, gram_ref, work_ref, inverse_ref, raw_ref, folded_ref):
    grads, rank, _ = work_ref.shape
    core = place_ref[0]
    chips = mine_ref.shape[0]
    part = raw_ref.shape[1] // (CORES * chips)
    piece = folded_ref.shape[1] // chips
    for chip in range(chips):
        for side, ref in enumerate((mine_ref, other_ref)):
            folded_ref[side, chip * piece:(chip + 1) * piece, :] = ref[chip, grads * part:, :]
    work_ref[...] = jnp.zeros(work_ref.shape, jnp.float32)
    unfold(work_ref, core, folded_ref, 0)
    unfold(work_ref, 1 - core, folded_ref, 1)
    for g in range(grads):
        place_rows(raw_ref, g, part, g, core, mine_ref, other_ref)
    invert_factor(work_ref, inverse_ref)
    for g in range(grads):
        out_ref[g] = exact(raw_ref[g], inverse_ref[g], FAR)
    chosen = out_ref[core]
    gram_ref[...] = exact(chosen, chosen, TALL)


def balance(place, mine, other, grads, depth):
    rank = mine.shape[2]
    return pl.pallas_call(
        balance_kernel,
        in_specs=[SMEM, VMEM, VMEM],
        out_specs=[VMEM, VMEM],
        out_shape=[jax.ShapeDtypeStruct((grads, depth, rank), jnp.float32), jax.ShapeDtypeStruct((rank, rank), jnp.float32)],
        scratch_shapes=[pltpu.VMEM((grads, rank, rank), jnp.float32)] * 2 + [pltpu.VMEM((grads, depth, rank), jnp.float32), pltpu.VMEM((2, 3 * rank // 4, rank), jnp.float32)],
        compiler_params=params(0),
    )(place, mine, other)


def project_kernel(scale, place_ref, order_ref, grad_ref, mine_ref, other_ref, balanced_ref, basis_ref, high_ref, low_ref, *refs):
    out_refs, (left_high, left_low, work_ref, inverse_ref) = refs[:-4], refs[-4:]
    grads, _, _ = high_ref.shape
    part = basis_ref.shape[1]
    core = place_ref[0]

    @pl.when(pl.program_id(0) == 0)
    def _():
        work_ref[core] = mine_ref[...]
        work_ref[1 - core] = other_ref[...]
        invert_factor(work_ref, inverse_ref)
        for g in range(grads):
            high_ref[g], low_ref[g] = split(exact(inverse_ref[g], balanced_ref[g], FAR))
            rows = balanced_ref[g, pl.ds(pl.multiple_of(place_ref[5] * part, part), part), :]
            basis_ref[g] = exact(rows, inverse_ref[g], FAR) * scale

    emit_quarter(order_ref, grad_ref, high_ref, low_ref, out_refs, left_high, left_low)


def project(place, order, gradients, mine, other, balanced, part, scale):
    grads, depth, width = gradients.shape
    rank = balanced.shape[2]
    _, out_specs, out_shape, scratch = quarter_shapes(gradients[:1], rank)
    shape, basis_shape = (grads, part, rank), (grads, rank, depth)
    return pl.pallas_call(
        functools.partial(project_kernel, scale),
        grid=(2,),
        in_specs=[SMEM, SMEM, pl.BlockSpec((1, depth, width // 2), lambda q: (0, 0, q)), full_block(mine.shape), full_block(other.shape), full_block(balanced.shape)],
        out_specs=[full_block(shape)] + [full_block(basis_shape)] * 2 + out_specs,
        out_shape=[jax.ShapeDtypeStruct(shape, jnp.float32)] + [jax.ShapeDtypeStruct(basis_shape, jnp.bfloat16)] * 2 + out_shape,
        scratch_shapes=scratch[2:] + [pltpu.VMEM((grads, rank, rank), jnp.float32)] * 2,
        compiler_params=params(1),
    )(place, order, gradients, mine, other, balanced)


def later_kernel(order_ref, grad_ref, high_ref, low_ref, *refs):
    emit_quarter(order_ref, grad_ref, high_ref, low_ref, refs[:-2], *refs[-2:])


def project_later(order, gradients, high, low, grad):
    _, depth, width = gradients.shape
    rank = high.shape[1]
    _, out_specs, out_shape, scratch = quarter_shapes(gradients[:1], rank)
    half = pl.BlockSpec((1, rank, depth), lambda q: (grad, 0, 0))
    return pl.pallas_call(
        later_kernel,
        grid=(2,),
        in_specs=[SMEM, pl.BlockSpec((1, depth, width // 2), lambda q: (grad, 0, q)), half, half],
        out_specs=out_specs,
        out_shape=out_shape,
        scratch_shapes=scratch[2:],
        compiler_params=params(1),
    )(order, gradients, high, low)


def swap_core(value):
    size = lax.axis_size("col")
    return lax.ppermute(value, "col", [(i, i ^ 1) for i in range(size)])


def chips_exchange(value):
    size = lax.axis_size("col")
    groups = [list(range(core, size, CORES)) for core in range(CORES)]
    return lax.all_to_all(value, "col", 0, 0, axis_index_groups=groups, tiled=True)


def spread(value, count):
    return jnp.broadcast_to(value[None], (count,) + value.shape)


def sum_columns(keep, send):
    mine = jnp.sum(chips_exchange(keep + swap_core(send)), 0)
    mine = chips_exchange(spread(mine, keep.shape[0]))
    return (mine, swap_core(mine))


def cube_partner(axis):
    pairs = []
    for y in range(SIDE):
        for x in range(SIDE):
            other = (y, x ^ 1), (y, SIDE - 1 - x), (y ^ 1, x), (SIDE - 1 - y, x)
            pairs.append((SIDE * y + x, SIDE * other[axis][0] + other[axis][1]))
    return pairs


def cube_bits(place):
    bits = []
    for digit in (place % SIDE, place // SIDE):
        bits += [(digit ^ (digit >> 1)) & 1, digit >> 1]
    return bits


def cube_order(quarter):
    return ORDERS[quarter % len(ORDERS)]


def cube_places(quarter):
    places = [0] * SIDE**2
    for place in range(SIDE**2):
        bits = cube_bits(place)
        position = 0
        for axis in cube_order(quarter):
            position = 2 * position + bits[axis]
        places[position] = place
    return places


def send_first(bits, tables, start=0):
    rows = []
    for quarter, table in enumerate(tables):
        low, high = jnp.array(table[:len(table) // 2], jnp.int32), jnp.array(table[len(table) // 2:], jnp.int32)
        bit = bits[cube_order(start + quarter)[0]]
        rows.append(jnp.concatenate([jnp.where(bit == 0, high, low), jnp.where(bit == 0, low, high)]))
    return jnp.stack(rows)


def across(value, quarter, step):
    return lax.ppermute(value, "row", cube_partner(cube_order(quarter)[step]))


def halves(value, bit):
    half = value.shape[0] // 2
    return (lax.dynamic_slice_in_dim(value, (1 - bit) * half, half, 0), lax.dynamic_slice_in_dim(value, bit * half, half, 0))


def scatter_sum(pairs, bits):
    numbers = list(range(len(pairs)))
    for step in range(4):
        sent = [across(away, q, step) for q, (away, kept) in zip(numbers, pairs)]
        if step == 3:
            return [kept + got for got, (away, kept) in zip(sent, pairs)]
        parts = []
        for q, got, (away, kept) in zip(numbers, sent, pairs):
            bit = bits[cube_order(q)[step + 1 if step != 1 else 2]]
            parts.append([mine + theirs for mine, theirs in zip(halves(kept, bit), halves(got, bit))])
        if step == 1:
            numbers = numbers[::2]
            parts = [[jnp.concatenate(both, 1) for both in zip(parts[q], parts[q + 1])] for q in numbers]
        pairs = parts


def gather(values, bits):
    numbers = list(range(0, 2 * len(values), 2))
    for step in (3, 2, 1, 0):
        got = [across(value, q, step) for q, value in zip(numbers, values)]
        if step == 0:
            return [piece for pair in zip(values, got) for piece in pair]
        wide = []
        for q, value, other in zip(numbers, values, got):
            high = bits[cube_order(q)[step]] == 1
            wide.append(jnp.concatenate([jnp.where(high, other, value), jnp.where(high, value, other)], 0))
        values = wide
        if step == 2:
            numbers = [number for q in numbers for number in (q, q + 1)]
            values = [piece for value in wide for piece in jnp.split(value, 2, 1)]


def shards(gradients, sketch):
    grads, depth, width = gradients.shape
    rank = sketch.shape[1]
    row_size, col_size = lax.axis_size("row"), lax.axis_size("col")
    chip_count = col_size // CORES
    part = depth // col_size
    total_rows = depth * row_size

    bits = cube_bits(lax.axis_index("row"))
    col = lax.axis_index("col")
    place = jnp.stack([col % CORES] + bits + [col]).astype(jnp.int32)
    plain = [send_first(bits, [list(range(row_size))] * 2, 2 * g) for g in range(grads)]
    final = [send_first(bits, [cube_places(q) for q in range(2 * g, 2 * g + 2)], 2 * g) for g in range(grads)]

    mine, other = sum_columns(*first_product(place, gradients, sketch, chip_count, part))
    outs = [piece for g in range(grads) for piece in pull(place, plain[g], gradients, mine, other, g)]
    quarters = scatter_sum([(outs[2 * q], outs[2 * q + 1]) for q in range(2 * grads)], bits)
    pieces = gather(quarters, bits)
    mine, other = sum_columns(*second_product(place, gradients, pieces, chip_count, part))

    balanced, gram_part = balance(place, mine, other, grads, depth)
    gram_mine = jnp.sum(lax.all_to_all(gram_part.reshape(row_size, rank // row_size, rank), "row", 0, 0, tiled=True), 0)
    gram = lax.all_to_all(spread(gram_mine, row_size), "row", 0, 0, tiled=True).reshape(rank, rank)

    basis, high, low, *outs = project(place, final[0], gradients, gram, swap_core(gram), balanced, part, float(total_rows) ** 0.5)
    outs = outs + [piece for g in range(1, grads) for piece in project_later(final[g], gradients, high, low, g)]
    quarters = scatter_sum([(outs[2 * q], outs[2 * q + 1]) for q in range(2 * grads)], bits)
    return (basis, jnp.stack(quarters))


def solution(mesh):
    in_specs = (P(None, "row", "col"), P("col", None))
    out_specs = (P(None, ("row", "col"), None), P(None, "row", "col"))
    return jax.shard_map(shards, mesh=mesh, in_specs=in_specs, out_specs=out_specs, check_vma=False)
```
